32 devices in a mesh: head: 2 (over x), ctx: 16 (over z, y, core).
Axes of the slice: x: 2, y: 2, z: 4, core: 2. Of those that a mesh axis runs over, the one named last changes fastest.
Arguments:
- queries: bfloat16 [2048, 6144], P('ctx', 'head'), may hold values from -6 to 6
- key_rows: bfloat16 [2048, 1024], P('ctx', 'head'), may hold values from -6 to 6
- value_rows: bfloat16 [2048, 1024], P('ctx', 'head'), may hold values from -6 to 6
- out_grad: bfloat16 [2048, 6144], P('ctx', 'head'), may hold values from -24 to 24
- gate_logit: float32 [2048], P('ctx'), may hold values from -6 to 6
- tile_plan: int32 [16, 4, 16], replicated, may hold values from -1 to 15, as said below
- mask_kind: int32 [16, 4, 16], P('ctx'), may hold values from 0 to 1
Outputs:
- query_grad: bfloat16 [2048, 6144], P('ctx', 'head')
- key_grad: bfloat16 [2048, 1024], P('ctx', 'head')
- value_grad: bfloat16 [2048, 1024], P('ctx', 'head')
- gate_grad: float32 [2048], P('ctx')
The draws below stay inside these ranges and needn't reach their ends.
Inputs may be any that keep to these rules, and one draw needn't show every extreme that they name: tile_plan[b, s, p] is a key tile of block p (of 8 rows) that block b reads in section s, or -1; it is -1 when p == b; the tiles that b reads from one p differ from section to section; in every section each block reads from between 4 and 8 blocks, and some block reads from exactly 8.
All inputs are finite; a program needn't handle non-finite values.
Results may differ from the reference program's by a relative error of at most 0.033.
Values may be sent and summed in bfloat16 or wider, within the bound.
A program may use at most 64 MiB of HBM per device.

```python
import math
import jax
import jax.numpy as jnp
from jax import lax

QH = 48
KVH = 8
HD = 128
ROWS = 128
TILE = 8
SECTIONS = 4
SEQ = 2048
PICKS = 8
N_CTX = 16


def draw_queries(key, part):
    blocks = SEQ // ROWS
    base_key = jax.random.fold_in(key, 11)
    field = jnp.clip(jax.random.normal(base_key, (SEQ, QH * HD), jnp.float32), -6.0, 6.0)
    field = field.reshape(blocks, ROWS, QH * HD)
    return field.reshape(SEQ, QH * HD).astype(jnp.bfloat16)


def draw_key_rows(key, part):
    blocks = SEQ // ROWS
    base_key = jax.random.fold_in(key, 12)
    field = jnp.clip(jax.random.normal(base_key, (SEQ, KVH * HD), jnp.float32), -6.0, 6.0)
    field = field.reshape(blocks, ROWS, KVH * HD)
    return field.reshape(SEQ, KVH * HD).astype(jnp.bfloat16)


def draw_out_grad(key, part):
    columns = QH * HD
    base_key = jax.random.fold_in(key, 13)
    field = jnp.clip(jax.random.normal(base_key, (SEQ, columns), jnp.float32), -4.0, 4.0)
    ratio = 3.0
    rough = jnp.exp(jax.random.uniform(jax.random.fold_in(key, 15), (columns,), jnp.float32, -0.35, 0.35))
    rising = ratio ** (jnp.arange(columns).astype(jnp.float32) / (columns - 1))
    return (field * rising[None, :] * rough[None, :]).astype(jnp.bfloat16)


def draw_tile_plan(key, part):
    blocks = SEQ // ROWS
    tile_count = ROWS // TILE
    first, second, third, fourth = jax.random.split(jax.random.fold_in(key, 14), 4)
    block_index = jnp.arange(blocks, dtype=jnp.int32)
    scores = jax.random.randint(first, (blocks, SECTIONS, blocks), 0, 1 << 20) * blocks + block_index[None, None, :]
    itself = block_index[:, None, None] == block_index[None, None, :]
    scores = jnp.where(itself, (1 << 20) * blocks + blocks, scores)
    ranking = jnp.argsort(jnp.argsort(scores, axis=-1), axis=-1)
    counts = jax.random.randint(second, (blocks, SECTIONS), blocks // 4, blocks // 2 + 1)
    filled = jax.random.randint(third, (SECTIONS,), 0, blocks)
    counts = jnp.where(block_index[:, None] == filled[None, :], blocks // 2, counts)
    chosen = ranking < counts[:, :, None]
    tile_scores = jax.random.randint(fourth, (blocks, blocks, tile_count), 0, 1 << 20) * tile_count + jnp.arange(tile_count)[None, None, :]
    tile_order = jnp.argsort(tile_scores, axis=-1)[:, :, :SECTIONS]
    tile_pick = jnp.transpose(tile_order, (0, 2, 1))
    return jnp.where(chosen, tile_pick, -1).astype(jnp.int32)


def place_ends(values, stream_key, low, largest):
    longest = values.shape.index(max(values.shape))
    spots = []
    for shift in (0, 1):
        where = [jax.random.randint(jax.random.fold_in(stream_key, axis), (), 0, length) for axis, length in enumerate(values.shape)]
        where[longest] = (where[longest] + shift) % values.shape[longest]
        spots.append(tuple(where))
    return values.at[spots[0]].set(low).at[spots[1]].set(largest)


def block_levels(own_key, extent, cuts, low, top_value):
    def one(axis_at, parts):
        heights = jax.random.uniform(jax.random.fold_in(jax.random.fold_in(own_key, 6), axis_at), (parts,), jnp.float32, low / len(cuts), top_value / len(cuts))
        return jnp.repeat(jnp.exp(heights), extent[axis_at] // parts).reshape((-1,) + (1,) * (len(extent) - axis_at - 1))

    gain = one(*cuts[0])
    for cut in cuts[1:]:
        gain = gain * one(*cut)
    return gain


def centred(rng, shape, scale, limit, pieces=(), kind=jnp.bfloat16):
    result = jax.random.normal(rng, shape, jnp.float32) * scale
    if len(pieces) > 0:
        result = block_levels(rng, shape, pieces, -0.22, 0.18) * result
    return jnp.clip(result, min=-limit, max=limit).astype(kind)


def setup_inputs(seed: int = 0) -> dict:
    key_list = jax.random.split(jax.random.key(seed), 8)
    return {
        "queries": draw_queries(jax.random.fold_in(key_list[7], 71), 0),
        "key_rows": draw_key_rows(jax.random.fold_in(key_list[7], 71), 0),
        "value_rows": centred(key_list[2], (SEQ, KVH * HD), 1.0, 6.0, ((0, 16), (1, 2))),
        "out_grad": draw_out_grad(jax.random.fold_in(key_list[7], 71), 0),
        "gate_logit": centred(key_list[4], (SEQ,), 1.5, 6.0, ((0, 16),), jnp.float32),
        "tile_plan": draw_tile_plan(jax.random.fold_in(key_list[7], 71), 0),
        "mask_kind": place_ends(jax.random.randint(key_list[6], (N_CTX, SECTIONS, N_CTX), 0, 2), jax.random.fold_in(key_list[6], 1), 0, 1).astype(jnp.int32),
    }


big_negative = -1e+30

def rounded(values):
    return lax.optimization_barrier(values.astype(jnp.bfloat16)).astype(jnp.float32)

def reference(queries, key_rows, value_rows, out_grad, gate_logit, tile_plan, mask_kind):
    blocks = SEQ // ROWS
    group_size = QH // KVH
    factor = 1.0 / math.sqrt(HD)
    gate = jax.nn.sigmoid(gate_logit.astype(jnp.float32))
    row_index = jnp.arange(ROWS, dtype=jnp.int32)
    tile_rows = jnp.arange(TILE, dtype=jnp.int32)
    late_rows = row_index >= ROWS // 2
    causal = row_index[:, None] >= row_index[None, :]
    key_float = key_rows.astype(jnp.float32).reshape(SEQ, KVH, HD)
    value_float = value_rows.astype(jnp.float32).reshape(SEQ, KVH, HD)

    def per_block(carry, index):
        key_total, value_total = carry
        start = (index * ROWS).astype(jnp.int32)
        query_block = lax.dynamic_slice_in_dim(queries, start, ROWS, 0).astype(jnp.float32).reshape(ROWS, KVH, group_size, HD)
        grad_block = lax.dynamic_slice_in_dim(out_grad, start, ROWS, 0).astype(jnp.float32).reshape(ROWS, KVH, group_size, HD)
        gate_block = lax.dynamic_slice_in_dim(gate, start, ROWS, 0)
        plan_row = tile_plan[index]
        kind_row = mask_kind[index]
        slot_order = jnp.argsort((plan_row < 0).astype(jnp.int32), axis=1, stable=True)[:, :PICKS].astype(jnp.int32)
        slot_tiles = jnp.take_along_axis(plan_row, slot_order, axis=1)
        slot_kinds = jnp.take_along_axis(kind_row, slot_order, axis=1)
        remote_rows = (slot_order * ROWS + jnp.maximum(slot_tiles, 0) * TILE)[:, :, None] + tile_rows
        all_rows = jnp.concatenate([start + row_index, remote_rows.reshape(-1).astype(jnp.int32)]).astype(jnp.int32)
        key_block = key_float[all_rows]
        value_block = value_float[all_rows]
        seen_tile = (slot_tiles >= 0)[None] & ((slot_kinds == 0)[None] | late_rows[:, None, None])
        seen_remote = jnp.broadcast_to(seen_tile[..., None], (ROWS, SECTIONS, PICKS, TILE)).reshape(ROWS, -1)
        visible = jnp.concatenate([causal, seen_remote], axis=1)
        scores = jnp.einsum('rcgd,kcd->cgrk', query_block, key_block) * factor
        masked = jnp.where(visible[None, None], scores, big_negative)
        highest = lax.optimization_barrier(jnp.max(masked, axis=-1, keepdims=True))
        log_total = highest + jnp.log(lax.optimization_barrier(jnp.sum(jnp.exp(masked - highest), axis=-1, keepdims=True)))
        probs = jnp.exp(masked - log_total)
        probs_low = rounded(probs)
        attended = rounded(jnp.einsum('cgrk,kcd->rcgd', probs_low, value_block))
        gate_sum = lax.optimization_barrier(jnp.sum(grad_block * attended, axis=(1, 2, 3)))
        gate_part = gate_block * (1.0 - gate_block) * gate_sum
        d_attended = rounded(gate_block[:, None, None, None] * grad_block)
        delta = jnp.transpose(lax.optimization_barrier(jnp.sum(d_attended * attended, axis=-1)), (1, 2, 0))
        d_probs = jnp.einsum('rcgd,kcd->cgrk', d_attended, value_block)
        d_scores = rounded(probs * (d_probs - delta[..., None]))
        query_part = jnp.einsum('cgrk,kcd->rcgd', d_scores, key_block) * factor
        key_part = jnp.einsum('cgrk,rcgd->kcd', d_scores, query_block) * factor
        value_part = jnp.einsum('cgrk,rcgd->kcd', probs_low, d_attended)
        key_total = key_total.at[all_rows].add(key_part.reshape(-1, KVH * HD))
        value_total = value_total.at[all_rows].add(value_part.reshape(-1, KVH * HD))
        query_out = query_part.reshape(ROWS, QH * HD).astype(jnp.bfloat16)
        return ((key_total, value_total), (query_out, gate_part))
    zeros_total = jnp.zeros((SEQ, KVH * HD), jnp.float32)
    totals, outputs = lax.scan(per_block, (zeros_total, zeros_total), jnp.arange(blocks, dtype=jnp.int32))
    query_grad = outputs[0].reshape(SEQ, QH * HD)
    gate_grad = outputs[1].reshape(SEQ)
    return (query_grad, totals[0].astype(jnp.bfloat16), totals[1].astype(jnp.bfloat16), gate_grad)
```

```python
import functools
import math

import jax
import jax.numpy as jnp
from jax import lax
from jax.experimental import pallas as pl
from jax.experimental.pallas import tpu as pltpu
from jax.sharding import PartitionSpec as P

HD = 128
TILE = 8
LINE = False

NEG = -1e30


def contract(a, b, dim_a, dim_b):
    return lax.dot_general(
        a, b, (((dim_a,), (dim_b,)), ((), ())), preferred_element_type=jnp.float32
    )


def kernel(
    peers,
    line_size,
    head_peers,
    q_ref,
    k_ref,
    v_ref,
    og_ref,
    gate_row_ref,
    gate_col_ref,
    plan_ref,
    kind_ref,
    dq_ref,
    dk_ref,
    dv_ref,
    dgate_ref,
    pick,
    bias,
    line,
    x_out,
    x_in,
    g_out,
    g_in,
    own_grad,
    q_rows,
    q_cols,
    da_rows,
    da_cols,
    og_cols,
    kv_all,
    probs_kept,
    scores_kept,
    gate_parts,
    r_send_buf,
    r_recv_buf,
    x_send,
    x_recv,
    g_send,
    g_recv,
    l_send,
    l_recv,
    r_send,
    r_recv,
    p_send,
    p_recv,
):
    rows = q_ref.shape[0]
    kv_count = k_ref.shape[1] // HD
    group = q_ref.shape[1] // k_ref.shape[1]
    width = group * HD
    sections = plan_ref.shape[1]
    spread = peers // line_size
    slot_rows = line_size * sections * TILE
    remote_rows = spread * slot_rows
    factor = 1.0 / math.sqrt(HD)
    me = lax.axis_index("ctx")
    place = me // spread
    lane_id = lax.rem(me, spread)
    head_id = lax.axis_index("head")

    def partner(offset):
        return lax.rem(lane_id + offset, spread)

    barrier = pltpu.get_barrier_semaphore()

    def greet(offset, carry):
        pl.semaphore_signal(barrier, inc=1, device_id={"ctx": place * spread + partner(offset)})
        return carry

    lax.fori_loop(1, spread, greet, 0)
    for offset in range(1, head_peers):
        pl.semaphore_signal(
            barrier, inc=1, device_id={"head": lax.rem(head_id + offset, head_peers)}
        )
    if line_size > 1:
        @pl.when(place > 0)
        def _():
            pl.semaphore_signal(barrier, inc=1, device_id={"ctx": me - spread})

        @pl.when(place < line_size - 1)
        def _():
            pl.semaphore_signal(barrier, inc=1, device_id={"ctx": me + spread})

    def columns(plan_rows, which):
        row = lax.broadcasted_iota(jnp.int32, (slot_rows, peers), 0)
        lane = lax.broadcasted_iota(jnp.int32, (slot_rows, peers), 1)
        hit = lane == (row // (sections * TILE)) * spread + which
        section = (row // TILE) % sections
        total = jnp.zeros((slot_rows, peers), jnp.float32)
        for index in range(sections):
            total = total + jnp.where(
                hit & (section == index), plan_rows[index : index + 1, :], 0.0
            )
        return jnp.sum(total, axis=1, keepdims=True)

    def build_pick(which, carry):
        plan_rows = plan_ref[place * spread + which].astype(jnp.float32)
        tile = columns(plan_rows, lane_id).astype(jnp.int32)
        shape = (slot_rows, line_size * rows)
        row = lax.broadcasted_iota(jnp.int32, shape, 0)
        lane = lax.broadcasted_iota(jnp.int32, shape, 1)
        target = (row // (sections * TILE)) * rows + tile * TILE + row % TILE
        pick[which] = jnp.where((tile >= 0) & (lane == target), 1.0, 0.0).astype(jnp.bfloat16)
        return carry

    lax.fori_loop(0, spread, build_pick, 0)

    def fill(head, carry):
        at = pl.ds(pl.multiple_of(head * HD, HD), HD)
        line[head, place] = jnp.concatenate([k_ref[:, at], v_ref[:, at]], axis=1)
        return carry

    lax.fori_loop(0, kv_count, fill, 0)

    waits = spread - 1 + head_peers - 1
    if waits > 0:
        pl.semaphore_wait(barrier, waits)
    if line_size > 1:
        @pl.when(place > 0)
        def _():
            pl.semaphore_wait(barrier, 1)

        @pl.when(place < line_size - 1)
        def _():
            pl.semaphore_wait(barrier, 1)

    def hop(head, way, step, origin):
        return pltpu.make_async_remote_copy(
            src_ref=line.at[head, origin],
            dst_ref=line.at[head, origin],
            send_sem=l_send.at[head, way, step],
            recv_sem=l_recv.at[head, way, step],
            device_id={"ctx": me + (spread if way == 0 else -spread)},
        )

    def hop_start(head, step):
        @pl.when((place >= step) & (place < line_size - 1))
        def _():
            hop(head, 0, step, place - step).start()

        @pl.when((place + step <= line_size - 1) & (place > 0))
        def _():
            hop(head, 1, step, place + step).start()

    def hop_wait(head, step):
        @pl.when(place - 1 - step >= 0)
        def _():
            hop(head, 0, step, place - 1 - step).wait_recv()

        @pl.when(place + 1 + step <= line_size - 1)
        def _():
            hop(head, 1, step, place + 1 + step).wait_recv()

    def hop_sent(head, step):
        @pl.when((place >= step) & (place < line_size - 1))
        def _():
            hop(head, 0, step, place - step).wait_send()

        @pl.when((place + step <= line_size - 1) & (place > 0))
        def _():
            hop(head, 1, step, place + step).wait_send()

    def exchange(source, target, send, recv, head, offset, slot):
        return pltpu.make_async_remote_copy(
            src_ref=source.at[head, partner(offset)],
            dst_ref=target.at[head, slot],
            send_sem=send.at[head, offset],
            recv_sem=recv.at[head, offset],
            device_id={"ctx": place * spread + partner(offset)},
        )

    def each(body):
        def step(offset, carry):
            body(offset)
            return carry

        lax.fori_loop(1, spread, step, 0)

    def front(head):
        for step in range(line_size - 1):
            hop_wait(head, step)
            if step + 1 < line_size - 1:
                hop_start(head, step + 1)
        flat = pick[...].reshape(remote_rows, line_size * rows)
        chosen = contract(flat, line[head].reshape(line_size * rows, 2 * HD), 1, 0)
        x_out[head] = chosen.astype(jnp.bfloat16).reshape(spread, slot_rows, 2 * HD)
        each(lambda o: exchange(x_out, x_in, x_send, x_recv, head, o, lane_id).start())
        x_in[head, lane_id] = x_out[head, lane_id]

    gate_row = jax.nn.sigmoid(gate_row_ref[...])
    gate_col = jax.nn.sigmoid(gate_col_ref[...])

    def prepare(head):
        for index in range(group):
            at = pl.ds(pl.multiple_of(head * width + index * HD, HD), HD)
            here = slice(index * HD, (index + 1) * HD)
            query = q_ref[:, at]
            grad = og_ref[:, at].astype(jnp.float32)
            grad_col = grad.T
            q_rows[head, here, :] = query
            q_cols[head, :, here] = query.astype(jnp.float32).T.astype(jnp.bfloat16)
            og_cols[head, :, here] = grad_col.astype(jnp.bfloat16)
            da_rows[head, here, :] = (gate_col * grad).astype(jnp.bfloat16)
            da_cols[head, :, here] = (gate_row * grad_col).astype(jnp.bfloat16)

    def build_bias():
        late = (
            lax.broadcasted_iota(jnp.int32, (slot_rows, rows), 1) >= rows // 2
        ).astype(jnp.float32)
        own_row = lax.broadcasted_iota(jnp.int32, (rows, rows), 0)
        own_lane = lax.broadcasted_iota(jnp.int32, (rows, rows), 1)
        bias[0:rows, :] = jnp.where(own_row <= own_lane, 0.0, NEG)
        seen = jnp.where(
            plan_ref[me] >= 0, 2.0 - kind_ref[0].astype(jnp.float32), 0.0
        )
        for which in range(spread):
            code = columns(seen, which)
            start = rows + which * slot_rows
            bias[start : start + slot_rows, :] = jnp.where(code + late >= 2.0, 0.0, NEG)

    pair = 2 if group % 2 == 0 else 1
    pair_width = pair * HD

    def middle(head):
        each(
            lambda o: exchange(
                x_out, x_in, x_send, x_recv, head, o, partner(spread - o)
            ).wait_recv()
        )
        kv_all[0:rows, :] = line[head, place]
        kv_all[rows:, :] = x_in[head].reshape(remote_rows, 2 * HD)
        keys = kv_all[:, 0:HD]
        values = kv_all[:, HD:]
        mask = jnp.concatenate([bias[...]] * pair, axis=1)
        for index in range(group // pair):
            here = slice(index * pair_width, (index + 1) * pair_width)
            scores = contract(keys, q_cols[head, :, here], 1, 0)
            scores = scores * (factor * math.log2(math.e)) + mask
            top = jnp.max(scores, axis=0, keepdims=True)
            probs = jnp.exp2(scores - top)
            probs = probs * (1.0 / jnp.sum(probs, axis=0, keepdims=True))
            probs_low = probs.astype(jnp.bfloat16)
            probs_kept[:, here] = probs_low
            attended = contract(values, probs_low, 0, 0)
            attended = attended.astype(jnp.bfloat16).astype(jnp.float32)
            da_here = da_cols[head, :, here]
            delta = jnp.sum(da_here.astype(jnp.float32) * attended, axis=0, keepdims=True)
            gate_term = jnp.sum(
                og_cols[head, :, here].astype(jnp.float32) * attended, axis=0, keepdims=True
            )
            for part in range(pair):
                term = gate_term[:, part * HD : (part + 1) * HD]
                gate_parts[head_id] += jnp.broadcast_to(term, (8, HD))
            d_probs = contract(values, da_here, 1, 0)
            scores_kept[head, :, here] = (probs * (d_probs - delta)).astype(jnp.bfloat16)
        d_values = contract(probs_kept[...], da_rows[head], 1, 0)
        d_keys = contract(scores_kept[head], q_rows[head], 1, 0) * factor
        both = jnp.concatenate([d_keys, d_values], axis=1)
        own_grad[head] = both[0:rows]
        g_out[head] = both[rows:].astype(jnp.bfloat16).reshape(spread, slot_rows, 2 * HD)
        each(lambda o: exchange(g_out, g_in, g_send, g_recv, head, o, lane_id).start())
        g_in[head, lane_id] = g_out[head, lane_id]
        kept_keys = kv_all[:, 0:HD]
        d_queries = contract(kept_keys, scores_kept[head], 0, 0) * factor
        for index in range(group):
            at = pl.ds(pl.multiple_of(head * width + index * HD, HD), HD)
            dq_ref[:, at] = d_queries[:, index * HD : (index + 1) * HD].T.astype(jnp.bfloat16)

    def chain(head, way, step):
        return pltpu.make_async_remote_copy(
            src_ref=r_send_buf.at[head, way, step],
            dst_ref=r_recv_buf.at[head, way, step],
            send_sem=r_send.at[head, way, step],
            recv_sem=r_recv.at[head, way, step],
            device_id={"ctx": me + (spread if way == 0 else -spread)},
        )

    def chain_roles(way, step):
        if way == 0:
            owner = line_size - 1 - step
            return owner, place < owner, place == 0
        owner = step
        return owner, place > owner, place == line_size - 1

    def back(head):
        each(
            lambda o: exchange(
                g_out, g_in, g_send, g_recv, head, o, partner(spread - o)
            ).wait_recv()
        )
        flat = pick[...].reshape(remote_rows, line_size * rows)
        dense = contract(flat, g_in[head].reshape(remote_rows, 2 * HD), 0, 0)
        if line_size > 1:
            for step in range(line_size - 1):
                for way in range(2):
                    owner, passes, first = chain_roles(way, step)
                    mine = dense[owner * rows : (owner + 1) * rows]

                    @pl.when(passes & first)
                    def _():
                        r_send_buf[head, way, step] = mine.astype(jnp.bfloat16)
                        chain(head, way, step).start()

                    @pl.when(passes & jnp.logical_not(first))
                    def _():
                        chain(head, way, step).wait_recv()
                        r_send_buf[head, way, step] = (
                            mine + r_recv_buf[head, way, step].astype(jnp.float32)
                        ).astype(jnp.bfloat16)
                        chain(head, way, step).start()

                    @pl.when(place == owner)
                    def _():
                        chain(head, way, step).wait_recv()
                        own_grad[head] += r_recv_buf[head, way, step].astype(jnp.float32)
            for owner in range(line_size):
                @pl.when(place == owner)
                def _():
                    own_grad[head] += dense[owner * rows : (owner + 1) * rows]
        else:
            own_grad[head] += dense
        at = pl.ds(pl.multiple_of(head * HD, HD), HD)
        dk_ref[:, at] = own_grad[head, :, 0:HD].astype(jnp.bfloat16)
        dv_ref[:, at] = own_grad[head, :, HD:].astype(jnp.bfloat16)

    gate_parts[head_id] = jnp.zeros((8, HD), jnp.float32)
    if line_size > 1:
        def begin(head, carry):
            hop_start(head, 0)
            return carry

        lax.fori_loop(0, kv_count, begin, 0)
    else:
        def begin(head, carry):
            front(head)
            return carry

        lax.fori_loop(0, kv_count, begin, 0)

    build_bias()

    def get_ready(head, carry):
        prepare(head)
        return carry

    lax.fori_loop(0, kv_count, get_ready, 0)

    def turn(step, carry):
        if line_size > 1:
            @pl.when(step < kv_count)
            def _():
                front(step)

        @pl.when((step >= 1) & (step <= kv_count))
        def _():
            middle(step - 1)

        @pl.when(step >= 2)
        def _():
            back(step - 2)

        return carry

    lax.fori_loop(0, kv_count + 1, turn, 0)

    def gate_copy(offset, slot):
        return pltpu.make_async_remote_copy(
            src_ref=gate_parts.at[head_id],
            dst_ref=gate_parts.at[slot],
            send_sem=p_send.at[offset],
            recv_sem=p_recv.at[offset],
            device_id={"head": lax.rem(head_id + offset, head_peers)},
        )

    for offset in range(1, head_peers):
        gate_copy(offset, head_id).start()
    back(kv_count - 1)
    for offset in range(1, head_peers):
        gate_copy(offset, lax.rem(head_id + head_peers - offset, head_peers)).wait_recv()
    total = jnp.sum(gate_parts[...], axis=0)
    dgate_ref[...] = gate_row * (1.0 - gate_row) * total[0:1, :]

    for offset in range(1, head_peers):
        gate_copy(offset, head_id).wait_send()

    def finish(head, carry):
        each(lambda o: exchange(x_out, x_in, x_send, x_recv, head, o, lane_id).wait_send())
        each(lambda o: exchange(g_out, g_in, g_send, g_recv, head, o, lane_id).wait_send())
        for step in range(line_size - 1):
            hop_sent(head, step)
            for way in range(2):
                _, passes, _ = chain_roles(way, step)

                @pl.when(passes)
                def _():
                    chain(head, way, step).wait_send()

        return carry

    lax.fori_loop(0, kv_count, finish, 0)


def solution(mesh):
    peers = mesh.shape["ctx"]
    head_peers = mesh.shape["head"]
    line_size = 1
    if LINE:
        while (line_size + 1) ** 2 <= peers:
            line_size += 1
        while peers % line_size:
            line_size -= 1
    spread = peers // line_size

    def body(queries, key_rows, value_rows, out_grad, gate_logit, tile_plan, mask_kind):
        rows = queries.shape[0]
        kv_count = key_rows.shape[1] // HD
        width = queries.shape[1] // kv_count
        sections = tile_plan.shape[1]
        slot_rows = line_size * sections * TILE
        key_count = rows + spread * slot_rows
        hops = max(line_size - 1, 1)
        low, full = jnp.bfloat16, jnp.float32
        vmem = pl.BlockSpec(memory_space=pltpu.VMEM)
        dma = pltpu.SemaphoreType.DMA
        outs = pl.pallas_call(
            functools.partial(kernel, peers, line_size, head_peers),
            out_shape=(
                jax.ShapeDtypeStruct(queries.shape, low),
                jax.ShapeDtypeStruct(key_rows.shape, low),
                jax.ShapeDtypeStruct(value_rows.shape, low),
                jax.ShapeDtypeStruct((1, rows), full),
            ),
            in_specs=[vmem] * 8,
            out_specs=(vmem,) * 4,
            scratch_shapes=[
                pltpu.VMEM((spread, slot_rows, line_size * rows), low),
                pltpu.VMEM((key_count, rows), full),
                pltpu.VMEM((kv_count, line_size, rows, 2 * HD), low),
                pltpu.VMEM((kv_count, spread, slot_rows, 2 * HD), low),
                pltpu.VMEM((kv_count, spread, slot_rows, 2 * HD), low),
                pltpu.VMEM((kv_count, spread, slot_rows, 2 * HD), low),
                pltpu.VMEM((kv_count, spread, slot_rows, 2 * HD), low),
                pltpu.VMEM((kv_count, rows, 2 * HD), full),
                pltpu.VMEM((kv_count, width, HD), low),
                pltpu.VMEM((kv_count, HD, width), low),
                pltpu.VMEM((kv_count, width, HD), low),
                pltpu.VMEM((kv_count, HD, width), low),
                pltpu.VMEM((kv_count, HD, width), low),
                pltpu.VMEM((key_count, 2 * HD), low),
                pltpu.VMEM((key_count, width), low),
                pltpu.VMEM((kv_count, key_count, width), low),
                pltpu.VMEM((head_peers, 8, rows), full),
                pltpu.VMEM((kv_count, 2, hops, rows, 2 * HD), low),
                pltpu.VMEM((kv_count, 2, hops, rows, 2 * HD), low),
                dma((kv_count, spread)),
                dma((kv_count, spread)),
                dma((kv_count, spread)),
                dma((kv_count, spread)),
                dma((kv_count, 2, hops)),
                dma((kv_count, 2, hops)),
                dma((kv_count, 2, hops)),
                dma((kv_count, 2, hops)),
                dma((head_peers,)),
                dma((head_peers,)),
            ],
            compiler_params=pltpu.CompilerParams(
                collective_id=0, has_side_effects=True, vmem_limit_bytes=56 * 1024 * 1024
            ),
            name="attention_grad",
        )(
            queries,
            key_rows,
            value_rows,
            out_grad,
            gate_logit.reshape(1, rows),
            gate_logit.reshape(rows, 1),
            tile_plan,
            mask_kind,
        )
        return outs[0], outs[1], outs[2], outs[3].reshape(rows)

    return jax.shard_map(
        body,
        mesh=mesh,
        in_specs=(
            P("ctx", "head"),
            P("ctx", "head"),
            P("ctx", "head"),
            P("ctx", "head"),
            P("ctx"),
            P(),
            P("ctx", None, None),
        ),
        out_specs=(P("ctx", "head"), P("ctx", "head"), P("ctx", "head"), P("ctx")),
        check_vma=False,
    )
```

```python
import functools
import math

import jax
import jax.numpy as jnp
from jax import lax
from jax.experimental import pallas as pl
from jax.experimental.pallas import tpu as pltpu
from jax.sharding import PartitionSpec as P

HD = 128
TILE = 8
LINE = True

NEG = -1e30


def contract(a, b, dim_a, dim_b):
    return lax.dot_general(
        a, b, (((dim_a,), (dim_b,)), ((), ())), preferred_element_type=jnp.float32
    )


def kernel(
    peers,
    line_size,
    head_peers,
    q_ref,
    k_ref,
    v_ref,
    og_ref,
    gate_row_ref,
    gate_col_ref,
    plan_ref,
    kind_ref,
    dq_ref,
    dk_ref,
    dv_ref,
    dgate_ref,
    pick,
    bias,
    line,
    x_out,
    x_in,
    g_out,
    g_in,
    own_grad,
    q_rows,
    q_cols,
    da_rows,
    da_cols,
    og_cols,
    kv_all,
    probs_kept,
    scores_kept,
    gate_parts,
    r_send_buf,
    r_recv_buf,
    x_send,
    x_recv,
    g_send,
    g_recv,
    l_send,
    l_recv,
    r_send,
    r_recv,
    p_send,
    p_recv,
):
    rows = q_ref.shape[0]
    kv_count = k_ref.shape[1] // HD
    group = q_ref.shape[1] // k_ref.shape[1]
    width = group * HD
    sections = plan_ref.shape[1]
    spread = peers // line_size
    slot_rows = line_size * sections * TILE
    remote_rows = spread * slot_rows
    factor = 1.0 / math.sqrt(HD)
    me = lax.axis_index("ctx")
    place = me // spread
    lane_id = lax.rem(me, spread)
    head_id = lax.axis_index("head")

    def partner(offset):
        return lax.rem(lane_id + offset, spread)

    barrier = pltpu.get_barrier_semaphore()

    def greet(offset, carry):
        pl.semaphore_signal(barrier, inc=1, device_id={"ctx": place * spread + partner(offset)})
        return carry

    lax.fori_loop(1, spread, greet, 0)
    for offset in range(1, head_peers):
        pl.semaphore_signal(
            barrier, inc=1, device_id={"head": lax.rem(head_id + offset, head_peers)}
        )
    if line_size > 1:
        @pl.when(place > 0)
        def _():
            pl.semaphore_signal(barrier, inc=1, device_id={"ctx": me - spread})

        @pl.when(place < line_size - 1)
        def _():
            pl.semaphore_signal(barrier, inc=1, device_id={"ctx": me + spread})

    def columns(plan_rows, which):
        row = lax.broadcasted_iota(jnp.int32, (slot_rows, peers), 0)
        lane = lax.broadcasted_iota(jnp.int32, (slot_rows, peers), 1)
        hit = lane == (row // (sections * TILE)) * spread + which
        section = (row // TILE) % sections
        total = jnp.zeros((slot_rows, peers), jnp.float32)
        for index in range(sections):
            total = total + jnp.where(
                hit & (section == index), plan_rows[index : index + 1, :], 0.0
            )
        return jnp.sum(total, axis=1, keepdims=True)

    def build_pick(which, carry):
        plan_rows = plan_ref[place * spread + which].astype(jnp.float32)
        tile = columns(plan_rows, lane_id).astype(jnp.int32)
        shape = (slot_rows, line_size * rows)
        row = lax.broadcasted_iota(jnp.int32, shape, 0)
        lane = lax.broadcasted_iota(jnp.int32, shape, 1)
        target = (row // (sections * TILE)) * rows + tile * TILE + row % TILE
        pick[which] = jnp.where((tile >= 0) & (lane == target), 1.0, 0.0).astype(jnp.bfloat16)
        return carry

    lax.fori_loop(0, spread, build_pick, 0)

    def fill(head, carry):
        at = pl.ds(pl.multiple_of(head * HD, HD), HD)
        line[head, place] = jnp.concatenate([k_ref[:, at], v_ref[:, at]], axis=1)
        return carry

    lax.fori_loop(0, kv_count, fill, 0)

    below = (place + line_size - 1) // line_size
    above = (2 * (line_size - 1) - place) // line_size
    pl.semaphore_wait(barrier, spread - 1 + head_peers - 1 + below + above)

    def hop(head, way, step, origin):
        return pltpu.make_async_remote_copy(
            src_ref=line.at[head, origin],
            dst_ref=line.at[head, origin],
            send_sem=l_send.at[head, way, step],
            recv_sem=l_recv.at[head, way, step],
            device_id={"ctx": me + (spread if way == 0 else -spread)},
        )

    def hop_start(head, step):
        @pl.when((place >= step) & (place < line_size - 1))
        def _():
            hop(head, 0, step, place - step).start()

        @pl.when((place + step <= line_size - 1) & (place > 0))
        def _():
            hop(head, 1, step, place + step).start()

    def hop_wait(head, step):
        @pl.when(place - 1 - step >= 0)
        def _():
            hop(head, 0, step, place - 1 - step).wait_recv()

        @pl.when(place + 1 + step <= line_size - 1)
        def _():
            hop(head, 1, step, place + 1 + step).wait_recv()

    def hop_sent(head, step):
        @pl.when((place >= step) & (place < line_size - 1))
        def _():
            hop(head, 0, step, place - step).wait_send()

        @pl.when((place + step <= line_size - 1) & (place > 0))
        def _():
            hop(head, 1, step, place + step).wait_send()

    def exchange(source, target, send, recv, head, offset, slot):
        return pltpu.make_async_remote_copy(
            src_ref=source.at[head, partner(offset)],
            dst_ref=target.at[head, slot],
            send_sem=send.at[head, offset],
            recv_sem=recv.at[head, offset],
            device_id={"ctx": place * spread + partner(offset)},
        )

    def each(body):
        def step(offset, carry):
            body(offset)
            return carry

        lax.fori_loop(1, spread, step, 0)

    def front(head):
        for step in range(line_size - 1):
            hop_wait(head, step)
            if step + 1 < line_size - 1:
                hop_start(head, step + 1)
        flat = pick[...].reshape(remote_rows, line_size * rows)
        chosen = contract(flat, line[head].reshape(line_size * rows, 2 * HD), 1, 0)
        x_out[head] = chosen.astype(jnp.bfloat16).reshape(spread, slot_rows, 2 * HD)
        each(lambda o: exchange(x_out, x_in, x_send, x_recv, head, o, lane_id).start())
        x_in[head, lane_id] = x_out[head, lane_id]

    gate_row = jax.nn.sigmoid(gate_row_ref[...])
    gate_col = jax.nn.sigmoid(gate_col_ref[...])

    def prepare(head):
        for index in range(group):
            at = pl.ds(pl.multiple_of(head * width + index * HD, HD), HD)
            here = slice(index * HD, (index + 1) * HD)
            query = q_ref[:, at]
            grad = og_ref[:, at].astype(jnp.float32)
            grad_col = grad.T
            q_rows[head, here, :] = query
            q_cols[head, :, here] = query.astype(jnp.float32).T.astype(jnp.bfloat16)
            og_cols[head, :, here] = grad_col.astype(jnp.bfloat16)
            da_rows[head, here, :] = (gate_col * grad).astype(jnp.bfloat16)
            da_cols[head, :, here] = (gate_row * grad_col).astype(jnp.bfloat16)

    def build_bias():
        late = (
            lax.broadcasted_iota(jnp.int32, (slot_rows, rows), 1) >= rows // 2
        ).astype(jnp.float32)
        own_row = lax.broadcasted_iota(jnp.int32, (rows, rows), 0)
        own_lane = lax.broadcasted_iota(jnp.int32, (rows, rows), 1)
        bias[0:rows, :] = jnp.where(own_row <= own_lane, 0.0, NEG)
        seen = jnp.where(
            plan_ref[me] >= 0, 2.0 - kind_ref[0].astype(jnp.float32), 0.0
        )
        for which in range(spread):
            code = columns(seen, which)
            start = rows + which * slot_rows
            bias[start : start + slot_rows, :] = jnp.where(code + late >= 2.0, 0.0, NEG)

    pair = 2 if group % 2 == 0 else 1
    pair_width = pair * HD

    def middle(head):
        each(
            lambda o: exchange(
                x_out, x_in, x_send, x_recv, head, o, partner(spread - o)
            ).wait_recv()
        )
        kv_all[0:rows, :] = line[head, place]
        kv_all[rows:, :] = x_in[head].reshape(remote_rows, 2 * HD)
        keys = kv_all[:, 0:HD]
        values = kv_all[:, HD:]
        mask = jnp.concatenate([bias[...]] * pair, axis=1)
        for index in range(group // pair):
            here = slice(index * pair_width, (index + 1) * pair_width)
            scores = contract(keys, q_cols[head, :, here], 1, 0)
            scores = scores * (factor * math.log2(math.e)) + mask
            top = jnp.max(scores, axis=0, keepdims=True)
            probs = jnp.exp2(scores - top)
            probs = probs * (1.0 / jnp.sum(probs, axis=0, keepdims=True))
            probs_low = probs.astype(jnp.bfloat16)
            probs_kept[:, here] = probs_low
            attended = contract(values, probs_low, 0, 0)
            attended = attended.astype(jnp.bfloat16).astype(jnp.float32)
            da_here = da_cols[head, :, here]
            delta = jnp.sum(da_here.astype(jnp.float32) * attended, axis=0, keepdims=True)
            gate_term = jnp.sum(
                og_cols[head, :, here].astype(jnp.float32) * attended, axis=0, keepdims=True
            )
            for part in range(pair):
                term = gate_term[:, part * HD : (part + 1) * HD]
                gate_parts[head_id] += jnp.broadcast_to(term, (8, HD))
            d_probs = contract(values, da_here, 1, 0)
            scores_kept[head, :, here] = (probs * (d_probs - delta)).astype(jnp.bfloat16)
        d_values = contract(probs_kept[...], da_rows[head], 1, 0)
        d_keys = contract(scores_kept[head], q_rows[head], 1, 0) * factor
        both = jnp.concatenate([d_keys, d_values], axis=1)
        own_grad[head] = both[0:rows]
        g_out[head] = both[rows:].astype(jnp.bfloat16).reshape(spread, slot_rows, 2 * HD)
        each(lambda o: exchange(g_out, g_in, g_send, g_recv, head, o, lane_id).start())
        g_in[head, lane_id] = g_out[head, lane_id]
        kept_keys = kv_all[:, 0:HD]
        d_queries = contract(kept_keys, scores_kept[head], 0, 0) * factor
        for index in range(group):
            at = pl.ds(pl.multiple_of(head * width + index * HD, HD), HD)
            dq_ref[:, at] = d_queries[:, index * HD : (index + 1) * HD].T.astype(jnp.bfloat16)

    def chain(head, way, step):
        return pltpu.make_async_remote_copy(
            src_ref=r_send_buf.at[head, way, step],
            dst_ref=r_recv_buf.at[head, way, step],
            send_sem=r_send.at[head, way, step],
            recv_sem=r_recv.at[head, way, step],
            device_id={"ctx": me + (spread if way == 0 else -spread)},
        )

    def chain_roles(way, step):
        if way == 0:
            owner = line_size - 1 - step
            return owner, place < owner, place == 0
        owner = step
        return owner, place > owner, place == line_size - 1

    def back(head):
        each(
            lambda o: exchange(
                g_out, g_in, g_send, g_recv, head, o, partner(spread - o)
            ).wait_recv()
        )
        flat = pick[...].reshape(remote_rows, line_size * rows)
        dense = contract(flat, g_in[head].reshape(remote_rows, 2 * HD), 0, 0)
        if line_size > 1:
            for step in range(line_size - 1):
                for way in range(2):
                    owner, passes, first = chain_roles(way, step)
                    mine = dense[owner * rows : (owner + 1) * rows]

                    @pl.when(passes & first)
                    def _():
                        r_send_buf[head, way, step] = mine.astype(jnp.bfloat16)
                        chain(head, way, step).start()

                    @pl.when(passes & jnp.logical_not(first))
                    def _():
                        chain(head, way, step).wait_recv()
                        r_send_buf[head, way, step] = (
                            mine + r_recv_buf[head, way, step].astype(jnp.float32)
                        ).astype(jnp.bfloat16)
                        chain(head, way, step).start()

                    @pl.when(place == owner)
                    def _():
                        chain(head, way, step).wait_recv()
                        own_grad[head] += r_recv_buf[head, way, step].astype(jnp.float32)
            for owner in range(line_size):
                @pl.when(place == owner)
                def _():
                    own_grad[head] += dense[owner * rows : (owner + 1) * rows]
        else:
            own_grad[head] += dense
        at = pl.ds(pl.multiple_of(head * HD, HD), HD)
        dk_ref[:, at] = own_grad[head, :, 0:HD].astype(jnp.bfloat16)
        dv_ref[:, at] = own_grad[head, :, HD:].astype(jnp.bfloat16)

    gate_parts[head_id] = jnp.zeros((8, HD), jnp.float32)
    if line_size > 1:
        def begin(head, carry):
            hop_start(head, 0)
            return carry

        lax.fori_loop(0, kv_count, begin, 0)
    else:
        def begin(head, carry):
            front(head)
            return carry

        lax.fori_loop(0, kv_count, begin, 0)

    build_bias()

    def get_ready(head, carry):
        prepare(head)
        return carry

    lax.fori_loop(0, kv_count, get_ready, 0)

    def turn(step, carry):
        if line_size > 1:
            @pl.when(step < kv_count)
            def _():
                front(step)

        @pl.when((step >= 1) & (step <= kv_count))
        def _():
            middle(step - 1)

        @pl.when(step >= 2)
        def _():
            back(step - 2)

        return carry

    lax.fori_loop(0, kv_count + 1, turn, 0)

    def gate_copy(offset, slot):
        return pltpu.make_async_remote_copy(
            src_ref=gate_parts.at[head_id],
            dst_ref=gate_parts.at[slot],
            send_sem=p_send.at[offset],
            recv_sem=p_recv.at[offset],
            device_id={"head": lax.rem(head_id + offset, head_peers)},
        )

    for offset in range(1, head_peers):
        gate_copy(offset, head_id).start()
    back(kv_count - 1)
    for offset in range(1, head_peers):
        gate_copy(offset, lax.rem(head_id + head_peers - offset, head_peers)).wait_recv()
    total = jnp.sum(gate_parts[...], axis=0)
    dgate_ref[...] = gate_row * (1.0 - gate_row) * total[0:1, :]

    for offset in range(1, head_peers):
        gate_copy(offset, head_id).wait_send()

    def finish(head, carry):
        each(lambda o: exchange(x_out, x_in, x_send, x_recv, head, o, lane_id).wait_send())
        each(lambda o: exchange(g_out, g_in, g_send, g_recv, head, o, lane_id).wait_send())
        for step in range(line_size - 1):
            hop_sent(head, step)
            for way in range(2):
                _, passes, _ = chain_roles(way, step)

                @pl.when(passes)
                def _():
                    chain(head, way, step).wait_send()

        return carry

    lax.fori_loop(0, kv_count, finish, 0)


def solution(mesh):
    peers = mesh.shape["ctx"]
    head_peers = mesh.shape["head"]
    line_size = 1
    if LINE:
        while (line_size + 1) ** 2 <= peers:
            line_size += 1
        while peers % line_size:
            line_size -= 1
    spread = peers // line_size

    def body(queries, key_rows, value_rows, out_grad, gate_logit, tile_plan, mask_kind):
        rows = queries.shape[0]
        kv_count = key_rows.shape[1] // HD
        width = queries.shape[1] // kv_count
        sections = tile_plan.shape[1]
        slot_rows = line_size * sections * TILE
        key_count = rows + spread * slot_rows
        hops = max(line_size - 1, 1)
        low, full = jnp.bfloat16, jnp.float32
        vmem = pl.BlockSpec(memory_space=pltpu.VMEM)
        dma = pltpu.SemaphoreType.DMA
        outs = pl.pallas_call(
            functools.partial(kernel, peers, line_size, head_peers),
            out_shape=(
                jax.ShapeDtypeStruct(queries.shape, low),
                jax.ShapeDtypeStruct(key_rows.shape, low),
                jax.ShapeDtypeStruct(value_rows.shape, low),
                jax.ShapeDtypeStruct((1, rows), full),
            ),
            in_specs=[vmem] * 8,
            out_specs=(vmem,) * 4,
            scratch_shapes=[
                pltpu.VMEM((spread, slot_rows, line_size * rows), low),
                pltpu.VMEM((key_count, rows), full),
                pltpu.VMEM((kv_count, line_size, rows, 2 * HD), low),
                pltpu.VMEM((kv_count, spread, slot_rows, 2 * HD), low),
                pltpu.VMEM((kv_count, spread, slot_rows, 2 * HD), low),
                pltpu.VMEM((kv_count, spread, slot_rows, 2 * HD), low),
                pltpu.VMEM((kv_count, spread, slot_rows, 2 * HD), low),
                pltpu.VMEM((kv_count, rows, 2 * HD), full),
                pltpu.VMEM((kv_count, width, HD), low),
                pltpu.VMEM((kv_count, HD, width), low),
                pltpu.VMEM((kv_count, width, HD), low),
                pltpu.VMEM((kv_count, HD, width), low),
                pltpu.VMEM((kv_count, HD, width), low),
                pltpu.VMEM((key_count, 2 * HD), low),
                pltpu.VMEM((key_count, width), low),
                pltpu.VMEM((kv_count, key_count, width), low),
                pltpu.VMEM((head_peers, 8, rows), full),
                pltpu.VMEM((kv_count, 2, hops, rows, 2 * HD), low),
                pltpu.VMEM((kv_count, 2, hops, rows, 2 * HD), low),
                dma((kv_count, spread)),
                dma((kv_count, spread)),
                dma((kv_count, spread)),
                dma((kv_count, spread)),
                dma((kv_count, 2, hops)),
                dma((kv_count, 2, hops)),
                dma((kv_count, 2, hops)),
                dma((kv_count, 2, hops)),
                dma((head_peers,)),
                dma((head_peers,)),
            ],
            compiler_params=pltpu.CompilerParams(
                collective_id=0, has_side_effects=True, vmem_limit_bytes=56 * 1024 * 1024
            ),
            name="attention_grad",
        )(
            queries,
            key_rows,
            value_rows,
            out_grad,
            gate_logit.reshape(1, rows),
            gate_logit.reshape(rows, 1),
            tile_plan,
            mask_kind,
        )
        return outs[0], outs[1], outs[2], outs[3].reshape(rows)

    return jax.shard_map(
        body,
        mesh=mesh,
        in_specs=(
            P("ctx", "head"),
            P("ctx", "head"),
            P("ctx", "head"),
            P("ctx", "head"),
            P("ctx"),
            P(),
            P("ctx", None, None),
        ),
        out_specs=(P("ctx", "head"), P("ctx", "head"), P("ctx", "head"), P("ctx")),
        check_vma=False,
    )
```

```python
import functools
import math

import jax
import jax.numpy as jnp
from jax import lax
from jax.experimental import pallas as pl
from jax.experimental.pallas import tpu as pltpu
from jax.sharding import PartitionSpec as P

HD = 128
TILE = 8
LINE = 2

NEG = -1e30


def contract(a, b, dim_a, dim_b):
    return lax.dot_general(
        a, b, (((dim_a,), (dim_b,)), ((), ())), preferred_element_type=jnp.float32
    )


def kernel(
    peers,
    line_size,
    head_peers,
    q_ref,
    k_ref,
    v_ref,
    og_ref,
    gate_row_ref,
    plan_ref,
    kind_ref,
    dq_ref,
    dk_ref,
    dv_ref,
    dgate_ref,
    pick,
    bias,
    line,
    x_out,
    x_in,
    g_out,
    g_in,
    own_grad,
    q_rows,
    q_cols,
    da_rows,
    da_cols,
    og_cols,
    kv_all,
    probs_kept,
    scores_kept,
    gate_parts,
    r_send_buf,
    r_recv_buf,
    x_send,
    x_recv,
    g_send,
    g_recv,
    l_send,
    l_recv,
    r_send,
    r_recv,
    p_send,
    p_recv,
):
    rows = q_ref.shape[0]
    kv_count = k_ref.shape[1] // HD
    group = q_ref.shape[1] // k_ref.shape[1]
    width = group * HD
    sections = plan_ref.shape[1]
    spread = peers // line_size
    slot_rows = line_size * sections * TILE
    remote_rows = spread * slot_rows
    factor = 1.0 / math.sqrt(HD)
    me = lax.axis_index("ctx")
    place = me // spread
    lane_id = lax.rem(me, spread)
    head_id = lax.axis_index("head")

    def partner(offset):
        return lax.rem(lane_id + offset, spread)

    barrier = pltpu.get_barrier_semaphore()

    def greet(offset, carry):
        pl.semaphore_signal(barrier, inc=1, device_id={"ctx": place * spread + partner(offset)})
        return carry

    lax.fori_loop(1, spread, greet, 0)
    for offset in range(1, head_peers):
        pl.semaphore_signal(
            barrier, inc=1, device_id={"head": lax.rem(head_id + offset, head_peers)}
        )
    if line_size > 1:
        @pl.when(place > 0)
        def _():
            pl.semaphore_signal(barrier, inc=1, device_id={"ctx": me - spread})

        @pl.when(place < line_size - 1)
        def _():
            pl.semaphore_signal(barrier, inc=1, device_id={"ctx": me + spread})

    def columns(plan_rows, which):
        row = lax.broadcasted_iota(jnp.int32, (slot_rows, peers), 0)
        lane = lax.broadcasted_iota(jnp.int32, (slot_rows, peers), 1)
        hit = lane == (row // (sections * TILE)) * spread + which
        section = (row // TILE) % sections
        total = jnp.zeros((slot_rows, peers), jnp.float32)
        for index in range(sections):
            total = total + jnp.where(
                hit & (section == index), plan_rows[index : index + 1, :], 0.0
            )
        return jnp.sum(total, axis=1, keepdims=True)

    def build_pick(which, carry):
        plan_rows = plan_ref[place * spread + which].astype(jnp.float32)
        tile = columns(plan_rows, lane_id).astype(jnp.int32)
        shape = (slot_rows, line_size * rows)
        row = lax.broadcasted_iota(jnp.int32, shape, 0)
        lane = lax.broadcasted_iota(jnp.int32, shape, 1)
        target = (row // (sections * TILE)) * rows + tile * TILE + row % TILE
        pick[which] = jnp.where((tile >= 0) & (lane == target), 1.0, 0.0).astype(jnp.bfloat16)
        return carry

    lax.fori_loop(0, spread, build_pick, 0)

    def fill(head, carry):
        at = pl.ds(pl.multiple_of(head * HD, HD), HD)
        line[head, place] = jnp.concatenate([k_ref[:, at], v_ref[:, at]], axis=1)
        return carry

    lax.fori_loop(0, kv_count, fill, 0)

    below = (place + line_size - 1) // line_size
    above = (2 * (line_size - 1) - place) // line_size
    pl.semaphore_wait(barrier, spread - 1 + head_peers - 1 + below + above)

    def hop(head, way, step, origin):
        return pltpu.make_async_remote_copy(
            src_ref=line.at[head, origin],
            dst_ref=line.at[head, origin],
            send_sem=l_send.at[head, way, step],
            recv_sem=l_recv.at[head, way, step],
            device_id={"ctx": me + (spread if way == 0 else -spread)},
        )

    def hop_start(head, step):
        @pl.when((place >= step) & (place < line_size - 1))
        def _():
            hop(head, 0, step, place - step).start()

        @pl.when((place + step <= line_size - 1) & (place > 0))
        def _():
            hop(head, 1, step, place + step).start()

    def hop_wait(head, step):
        @pl.when(place - 1 - step >= 0)
        def _():
            hop(head, 0, step, place - 1 - step).wait_recv()

        @pl.when(place + 1 + step <= line_size - 1)
        def _():
            hop(head, 1, step, place + 1 + step).wait_recv()

    def hop_sent(head, step):
        @pl.when((place >= step) & (place < line_size - 1))
        def _():
            hop(head, 0, step, place - step).wait_send()

        @pl.when((place + step <= line_size - 1) & (place > 0))
        def _():
            hop(head, 1, step, place + step).wait_send()

    def exchange(source, target, send, recv, head, offset, slot):
        return pltpu.make_async_remote_copy(
            src_ref=source.at[head, partner(offset)],
            dst_ref=target.at[head, slot],
            send_sem=send.at[head, offset],
            recv_sem=recv.at[head, offset],
            device_id={"ctx": place * spread + partner(offset)},
        )

    def each(body):
        def step(offset, carry):
            body(offset)
            return carry

        lax.fori_loop(1, spread, step, 0)

    def front(head):
        for step in range(line_size - 1):
            hop_wait(head, step)
            if step + 1 < line_size - 1:
                hop_start(head, step + 1)
        flat = pick[...].reshape(remote_rows, line_size * rows)
        chosen = contract(flat, line[head].reshape(line_size * rows, 2 * HD), 1, 0)
        x_out[head] = chosen.astype(jnp.bfloat16).reshape(spread, slot_rows, 2 * HD)
        each(lambda o: exchange(x_out, x_in, x_send, x_recv, head, o, lane_id).start())
        x_in[head, lane_id] = x_out[head, lane_id]

    gate_row = jax.nn.sigmoid(gate_row_ref[...])
    gate_col = jnp.broadcast_to(gate_row, (HD, rows)).T

    def prepare(head):
        for index in range(group):
            at = pl.ds(pl.multiple_of(head * width + index * HD, HD), HD)
            here = slice(index * HD, (index + 1) * HD)
            query = q_ref[:, at]
            grad = og_ref[:, at].astype(jnp.float32)
            grad_col = grad.T
            q_rows[head, here, :] = query
            q_cols[head, :, here] = query.astype(jnp.float32).T.astype(jnp.bfloat16)
            og_cols[head, :, here] = grad_col.astype(jnp.bfloat16)
            da_rows[head, here, :] = (gate_col * grad).astype(jnp.bfloat16)
            da_cols[head, :, here] = (gate_row * grad_col).astype(jnp.bfloat16)

    def build_bias():
        late = (
            lax.broadcasted_iota(jnp.int32, (slot_rows, rows), 1) >= rows // 2
        ).astype(jnp.float32)
        own_row = lax.broadcasted_iota(jnp.int32, (rows, rows), 0)
        own_lane = lax.broadcasted_iota(jnp.int32, (rows, rows), 1)
        bias[0:rows, :] = jnp.where(own_row <= own_lane, 0.0, NEG)
        seen = jnp.where(
            plan_ref[me] >= 0, 2.0 - kind_ref[0].astype(jnp.float32), 0.0
        )
        for which in range(spread):
            code = columns(seen, which)
            start = rows + which * slot_rows
            bias[start : start + slot_rows, :] = jnp.where(code + late >= 2.0, 0.0, NEG)

    pair = 2 if group % 2 == 0 else 1
    pair_width = pair * HD

    def middle(head):
        each(
            lambda o: exchange(
                x_out, x_in, x_send, x_recv, head, o, partner(spread - o)
            ).wait_recv()
        )
        kv_all[0:rows, :] = line[head, place]
        kv_all[rows:, :] = x_in[head].reshape(remote_rows, 2 * HD)
        keys = kv_all[:, 0:HD]
        values = kv_all[:, HD:]
        mask = jnp.concatenate([bias[...]] * pair, axis=1)
        for index in range(group // pair):
            here = slice(index * pair_width, (index + 1) * pair_width)
            scores = contract(keys, q_cols[head, :, here], 1, 0)
            scores = scores * (factor * math.log2(math.e)) + mask
            top = jnp.max(scores, axis=0, keepdims=True)
            probs = jnp.exp2(scores - top)
            probs = probs * (1.0 / jnp.sum(probs, axis=0, keepdims=True))
            probs_low = probs.astype(jnp.bfloat16)
            probs_kept[:, here] = probs_low
            attended = contract(values, probs_low, 0, 0)
            attended = attended.astype(jnp.bfloat16).astype(jnp.float32)
            da_here = da_cols[head, :, here]
            delta = jnp.sum(da_here.astype(jnp.float32) * attended, axis=0, keepdims=True)
            gate_term = jnp.sum(
                og_cols[head, :, here].astype(jnp.float32) * attended, axis=0, keepdims=True
            )
            for part in range(pair):
                term = gate_term[:, part * HD : (part + 1) * HD]
                gate_parts[head_id] += jnp.broadcast_to(term, (8, HD))
            d_probs = contract(values, da_here, 1, 0)
            scores_kept[head, :, here] = (probs * (d_probs - delta)).astype(jnp.bfloat16)
        d_values = contract(probs_kept[...], da_rows[head], 1, 0)
        d_keys = contract(scores_kept[head], q_rows[head], 1, 0) * factor
        both = jnp.concatenate([d_keys, d_values], axis=1)
        own_grad[head] = both[0:rows]
        g_out[head] = both[rows:].astype(jnp.bfloat16).reshape(spread, slot_rows, 2 * HD)
        each(lambda o: exchange(g_out, g_in, g_send, g_recv, head, o, lane_id).start())
        g_in[head, lane_id] = g_out[head, lane_id]
        kept_keys = kv_all[:, 0:HD]
        d_queries = contract(kept_keys, scores_kept[head], 0, 0) * factor
        dq_ref[head] = d_queries.astype(jnp.bfloat16)

    def chain(head, way, step):
        return pltpu.make_async_remote_copy(
            src_ref=r_send_buf.at[head, way, step],
            dst_ref=r_recv_buf.at[head, way, step],
            send_sem=r_send.at[head, way, step],
            recv_sem=r_recv.at[head, way, step],
            device_id={"ctx": me + (spread if way == 0 else -spread)},
        )

    def chain_roles(way, step):
        if way == 0:
            owner = line_size - 1 - step
            return owner, place < owner, place == 0
        owner = step
        return owner, place > owner, place == line_size - 1

    def back(head):
        each(
            lambda o: exchange(
                g_out, g_in, g_send, g_recv, head, o, partner(spread - o)
            ).wait_recv()
        )
        flat = pick[...].reshape(remote_rows, line_size * rows)
        dense = contract(flat, g_in[head].reshape(remote_rows, 2 * HD), 0, 0)
        if line_size > 1:
            for step in range(line_size - 1):
                for way in range(2):
                    owner, passes, first = chain_roles(way, step)
                    mine = dense[owner * rows : (owner + 1) * rows]

                    @pl.when(passes & first)
                    def _():
                        r_send_buf[head, way, step] = mine.astype(jnp.bfloat16)
                        chain(head, way, step).start()

                    @pl.when(passes & jnp.logical_not(first))
                    def _():
                        chain(head, way, step).wait_recv()
                        r_send_buf[head, way, step] = (
                            mine + r_recv_buf[head, way, step].astype(jnp.float32)
                        ).astype(jnp.bfloat16)
                        chain(head, way, step).start()

                    @pl.when(place == owner)
                    def _():
                        chain(head, way, step).wait_recv()
                        own_grad[head] += r_recv_buf[head, way, step].astype(jnp.float32)
            for owner in range(line_size):
                @pl.when(place == owner)
                def _():
                    own_grad[head] += dense[owner * rows : (owner + 1) * rows]
        else:
            own_grad[head] += dense
        at = pl.ds(pl.multiple_of(head * HD, HD), HD)
        dk_ref[:, at] = own_grad[head, :, 0:HD].astype(jnp.bfloat16)
        dv_ref[:, at] = own_grad[head, :, HD:].astype(jnp.bfloat16)

    gate_parts[head_id] = jnp.zeros((8, HD), jnp.float32)
    if line_size > 1:
        def begin(head, carry):
            hop_start(head, 0)
            return carry

        lax.fori_loop(0, kv_count, begin, 0)
    else:
        def begin(head, carry):
            front(head)
            return carry

        lax.fori_loop(0, kv_count, begin, 0)

    build_bias()

    def get_ready(head, carry):
        prepare(head)
        return carry

    lax.fori_loop(0, kv_count, get_ready, 0)

    def turn(step, carry):
        if line_size > 1:
            @pl.when(step < kv_count)
            def _():
                front(step)

        @pl.when((step >= 1) & (step <= kv_count))
        def _():
            middle(step - 1)

        @pl.when(step >= 2)
        def _():
            back(step - 2)

        return carry

    lax.fori_loop(0, kv_count + 1, turn, 0)

    def gate_copy(offset, slot):
        return pltpu.make_async_remote_copy(
            src_ref=gate_parts.at[head_id],
            dst_ref=gate_parts.at[slot],
            send_sem=p_send.at[offset],
            recv_sem=p_recv.at[offset],
            device_id={"head": lax.rem(head_id + offset, head_peers)},
        )

    for offset in range(1, head_peers):
        gate_copy(offset, head_id).start()
    back(kv_count - 1)
    for offset in range(1, head_peers):
        gate_copy(offset, lax.rem(head_id + head_peers - offset, head_peers)).wait_recv()
    total = jnp.sum(gate_parts[...], axis=0)
    dgate_ref[...] = gate_row * (1.0 - gate_row) * total[0:1, :]

    for offset in range(1, head_peers):
        gate_copy(offset, head_id).wait_send()

    def finish(head, carry):
        each(lambda o: exchange(x_out, x_in, x_send, x_recv, head, o, lane_id).wait_send())
        each(lambda o: exchange(g_out, g_in, g_send, g_recv, head, o, lane_id).wait_send())
        for step in range(line_size - 1):
            hop_sent(head, step)
            for way in range(2):
                _, passes, _ = chain_roles(way, step)

                @pl.when(passes)
                def _():
                    chain(head, way, step).wait_send()

        return carry

    lax.fori_loop(0, kv_count, finish, 0)


def write(dq_cols_ref, dk_in_ref, dv_in_ref, dgate_in_ref, dq_ref, dk_ref, dv_ref, dgate_ref):
    kv_count, _, width = dq_cols_ref.shape
    for head in range(kv_count):
        for index in range(width // HD):
            start = head * width + index * HD
            part = dq_cols_ref[head, :, index * HD : (index + 1) * HD]
            dq_ref[:, start : start + HD] = part.T
    dk_ref[...] = dk_in_ref[...]
    dv_ref[...] = dv_in_ref[...]
    dgate_ref[...] = dgate_in_ref[...]


def solution(mesh):
    peers = mesh.shape["ctx"]
    head_peers = mesh.shape["head"]
    line_size = LINE if peers % LINE == 0 else 1
    spread = peers // line_size

    def body(queries, key_rows, value_rows, out_grad, gate_logit, tile_plan, mask_kind):
        rows = queries.shape[0]
        kv_count = key_rows.shape[1] // HD
        width = queries.shape[1] // kv_count
        sections = tile_plan.shape[1]
        slot_rows = line_size * sections * TILE
        key_count = rows + spread * slot_rows
        hops = max(line_size - 1, 1)
        low, full = jnp.bfloat16, jnp.float32
        vmem = pl.BlockSpec(memory_space=pltpu.VMEM)
        dma = pltpu.SemaphoreType.DMA
        outs = pl.pallas_call(
            functools.partial(kernel, peers, line_size, head_peers),
            out_shape=(
                jax.ShapeDtypeStruct((kv_count, HD, width), low),
                jax.ShapeDtypeStruct(key_rows.shape, low),
                jax.ShapeDtypeStruct(value_rows.shape, low),
                jax.ShapeDtypeStruct((1, rows), full),
            ),
            in_specs=[vmem] * 7,
            out_specs=(vmem,) * 4,
            scratch_shapes=[
                pltpu.VMEM((spread, slot_rows, line_size * rows), low),
                pltpu.VMEM((key_count, rows), full),
                pltpu.VMEM((kv_count, line_size, rows, 2 * HD), low),
                pltpu.VMEM((kv_count, spread, slot_rows, 2 * HD), low),
                pltpu.VMEM((kv_count, spread, slot_rows, 2 * HD), low),
                pltpu.VMEM((kv_count, spread, slot_rows, 2 * HD), low),
                pltpu.VMEM((kv_count, spread, slot_rows, 2 * HD), low),
                pltpu.VMEM((kv_count, rows, 2 * HD), full),
                pltpu.VMEM((kv_count, width, HD), low),
                pltpu.VMEM((kv_count, HD, width), low),
                pltpu.VMEM((kv_count, width, HD), low),
                pltpu.VMEM((kv_count, HD, width), low),
                pltpu.VMEM((kv_count, HD, width), low),
                pltpu.VMEM((key_count, 2 * HD), low),
                pltpu.VMEM((key_count, width), low),
                pltpu.VMEM((kv_count, key_count, width), low),
                pltpu.VMEM((head_peers, 8, rows), full),
                pltpu.VMEM((kv_count, 2, hops, rows, 2 * HD), low),
                pltpu.VMEM((kv_count, 2, hops, rows, 2 * HD), low),
                dma((kv_count, spread)),
                dma((kv_count, spread)),
                dma((kv_count, spread)),
                dma((kv_count, spread)),
                dma((kv_count, 2, hops)),
                dma((kv_count, 2, hops)),
                dma((kv_count, 2, hops)),
                dma((kv_count, 2, hops)),
                dma((head_peers,)),
                dma((head_peers,)),
            ],
            compiler_params=pltpu.CompilerParams(
                collective_id=0, has_side_effects=True, vmem_limit_bytes=56 * 1024 * 1024
            ),
            name="attention_grad",
        )(
            queries,
            key_rows,
            value_rows,
            out_grad,
            gate_logit.reshape(1, rows),
            tile_plan,
            mask_kind,
        )
        outs = pl.pallas_call(
            write,
            out_shape=(
                jax.ShapeDtypeStruct(queries.shape, low),
                jax.ShapeDtypeStruct(key_rows.shape, low),
                jax.ShapeDtypeStruct(value_rows.shape, low),
                jax.ShapeDtypeStruct((1, rows), full),
            ),
            in_specs=[vmem] * 4,
            out_specs=(vmem,) * 4,
            name="write_grads",
        )(*outs)
        return outs[0], outs[1], outs[2], outs[3].reshape(rows)

    return jax.shard_map(
        body,
        mesh=mesh,
        in_specs=(
            P("ctx", "head"),
            P("ctx", "head"),
            P("ctx", "head"),
            P("ctx", "head"),
            P("ctx"),
            P(),
            P("ctx", None, None),
        ),
        out_specs=(P("ctx", "head"), P("ctx", "head"), P("ctx", "head"), P("ctx")),
        check_vma=False,
    )
```

```python
import functools
import math

import jax
import jax.numpy as jnp
from jax import lax
from jax.experimental import pallas as pl
from jax.experimental.pallas import tpu as pltpu
from jax.sharding import PartitionSpec as P

HD = 128
TILE = 8
LINE = 1

NEG = -1e30


def contract(a, b, dim_a, dim_b):
    return lax.dot_general(
        a, b, (((dim_a,), (dim_b,)), ((), ())), preferred_element_type=jnp.float32
    )


def kernel(
    peers,
    line_size,
    head_peers,
    q_ref,
    k_ref,
    v_ref,
    og_ref,
    gate_row_ref,
    plan_ref,
    kind_ref,
    dq_ref,
    dk_ref,
    dv_ref,
    dgate_ref,
    pick,
    bias,
    line,
    x_out,
    x_in,
    g_out,
    g_in,
    own_grad,
    q_rows,
    q_cols,
    da_rows,
    da_cols,
    og_cols,
    kv_all,
    probs_kept,
    scores_kept,
    gate_parts,
    r_send_buf,
    r_recv_buf,
    x_send,
    x_recv,
    g_send,
    g_recv,
    l_send,
    l_recv,
    r_send,
    r_recv,
    p_send,
    p_recv,
):
    rows = q_ref.shape[0]
    kv_count = k_ref.shape[1] // HD
    group = q_ref.shape[1] // k_ref.shape[1]
    width = group * HD
    sections = plan_ref.shape[1]
    spread = peers // line_size
    slot_rows = line_size * sections * TILE
    remote_rows = spread * slot_rows
    factor = 1.0 / math.sqrt(HD)
    me = lax.axis_index("ctx")
    place = me // spread
    lane_id = lax.rem(me, spread)
    head_id = lax.axis_index("head")

    def partner(offset):
        return lax.rem(lane_id + offset, spread)

    barrier = pltpu.get_barrier_semaphore()

    def greet(offset, carry):
        pl.semaphore_signal(barrier, inc=1, device_id={"ctx": place * spread + partner(offset)})
        return carry

    lax.fori_loop(1, spread, greet, 0)
    for offset in range(1, head_peers):
        pl.semaphore_signal(
            barrier, inc=1, device_id={"head": lax.rem(head_id + offset, head_peers)}
        )
    if line_size > 1:
        @pl.when(place > 0)
        def _():
            pl.semaphore_signal(barrier, inc=1, device_id={"ctx": me - spread})

        @pl.when(place < line_size - 1)
        def _():
            pl.semaphore_signal(barrier, inc=1, device_id={"ctx": me + spread})

    def columns(plan_rows, which):
        row = lax.broadcasted_iota(jnp.int32, (slot_rows, peers), 0)
        lane = lax.broadcasted_iota(jnp.int32, (slot_rows, peers), 1)
        hit = lane == (row // (sections * TILE)) * spread + which
        section = (row // TILE) % sections
        total = jnp.zeros((slot_rows, peers), jnp.float32)
        for index in range(sections):
            total = total + jnp.where(
                hit & (section == index), plan_rows[index : index + 1, :], 0.0
            )
        return jnp.sum(total, axis=1, keepdims=True)

    def build_pick(which, carry):
        plan_rows = plan_ref[place * spread + which].astype(jnp.float32)
        tile = columns(plan_rows, lane_id).astype(jnp.int32)
        shape = (slot_rows, line_size * rows)
        row = lax.broadcasted_iota(jnp.int32, shape, 0)
        lane = lax.broadcasted_iota(jnp.int32, shape, 1)
        target = (row // (sections * TILE)) * rows + tile * TILE + row % TILE
        pick[which] = jnp.where((tile >= 0) & (lane == target), 1.0, 0.0).astype(jnp.bfloat16)
        return carry

    lax.fori_loop(0, spread, build_pick, 0)

    def fill(head, carry):
        at = pl.ds(pl.multiple_of(head * HD, HD), HD)
        line[head, place] = jnp.concatenate([k_ref[:, at], v_ref[:, at]], axis=1)
        return carry

    lax.fori_loop(0, kv_count, fill, 0)

    below = (place + line_size - 1) // line_size
    above = (2 * (line_size - 1) - place) // line_size
    pl.semaphore_wait(barrier, spread - 1 + head_peers - 1 + below + above)

    def hop(head, way, step, origin):
        return pltpu.make_async_remote_copy(
            src_ref=line.at[head, origin],
            dst_ref=line.at[head, origin],
            send_sem=l_send.at[head, way, step],
            recv_sem=l_recv.at[head, way, step],
            device_id={"ctx": me + (spread if way == 0 else -spread)},
        )

    def hop_start(head, step):
        @pl.when((place >= step) & (place < line_size - 1))
        def _():
            hop(head, 0, step, place - step).start()

        @pl.when((place + step <= line_size - 1) & (place > 0))
        def _():
            hop(head, 1, step, place + step).start()

    def hop_wait(head, step):
        @pl.when(place - 1 - step >= 0)
        def _():
            hop(head, 0, step, place - 1 - step).wait_recv()

        @pl.when(place + 1 + step <= line_size - 1)
        def _():
            hop(head, 1, step, place + 1 + step).wait_recv()

    def hop_sent(head, step):
        @pl.when((place >= step) & (place < line_size - 1))
        def _():
            hop(head, 0, step, place - step).wait_send()

        @pl.when((place + step <= line_size - 1) & (place > 0))
        def _():
            hop(head, 1, step, place + step).wait_send()

    def exchange(source, target, send, recv, head, offset, slot):
        return pltpu.make_async_remote_copy(
            src_ref=source.at[head, partner(offset)],
            dst_ref=target.at[head, slot],
            send_sem=send.at[head, offset],
            recv_sem=recv.at[head, offset],
            device_id={"ctx": place * spread + partner(offset)},
        )

    def each(body):
        def step(offset, carry):
            body(offset)
            return carry

        lax.fori_loop(1, spread, step, 0)

    def front(head):
        for step in range(line_size - 1):
            hop_wait(head, step)
            if step + 1 < line_size - 1:
                hop_start(head, step + 1)
        flat = pick[...].reshape(remote_rows, line_size * rows)
        chosen = contract(flat, line[head].reshape(line_size * rows, 2 * HD), 1, 0)
        x_out[head] = chosen.astype(jnp.bfloat16).reshape(spread, slot_rows, 2 * HD)
        each(lambda o: exchange(x_out, x_in, x_send, x_recv, head, o, lane_id).start())
        x_in[head, lane_id] = x_out[head, lane_id]

    gate_row = jax.nn.sigmoid(gate_row_ref[...])
    gate_col = jnp.broadcast_to(gate_row, (HD, rows)).T

    def prepare(head):
        for index in range(group):
            at = pl.ds(pl.multiple_of(head * width + index * HD, HD), HD)
            here = slice(index * HD, (index + 1) * HD)
            query = q_ref[:, at]
            grad = og_ref[:, at].astype(jnp.float32)
            grad_col = grad.T
            q_rows[head, here, :] = query
            q_cols[head, :, here] = query.astype(jnp.float32).T.astype(jnp.bfloat16)
            og_cols[head, :, here] = grad_col.astype(jnp.bfloat16)
            da_rows[head, here, :] = (gate_col * grad).astype(jnp.bfloat16)
            da_cols[head, :, here] = (gate_row * grad_col).astype(jnp.bfloat16)

    def build_bias():
        late = (
            lax.broadcasted_iota(jnp.int32, (slot_rows, rows), 1) >= rows // 2
        ).astype(jnp.float32)
        own_row = lax.broadcasted_iota(jnp.int32, (rows, rows), 0)
        own_lane = lax.broadcasted_iota(jnp.int32, (rows, rows), 1)
        bias[0:rows, :] = jnp.where(own_row <= own_lane, 0.0, NEG)
        seen = jnp.where(
            plan_ref[me] >= 0, 2.0 - kind_ref[0].astype(jnp.float32), 0.0
        )
        for which in range(spread):
            code = columns(seen, which)
            start = rows + which * slot_rows
            bias[start : start + slot_rows, :] = jnp.where(code + late >= 2.0, 0.0, NEG)

    pair = 2 if group % 2 == 0 else 1
    pair_width = pair * HD

    def middle(head):
        each(
            lambda o: exchange(
                x_out, x_in, x_send, x_recv, head, o, partner(spread - o)
            ).wait_recv()
        )
        kv_all[head, 0:rows, :] = line[head, place]
        kv_all[head, rows:, :] = x_in[head].reshape(remote_rows, 2 * HD)
        keys = kv_all[head, :, 0:HD]
        values = kv_all[head, :, HD:]
        mask = jnp.concatenate([bias[...]] * pair, axis=1)
        for index in range(group // pair):
            here = slice(index * pair_width, (index + 1) * pair_width)
            scores = contract(keys, q_cols[head, :, here], 1, 0)
            scores = scores * (factor * math.log2(math.e)) + mask
            top = jnp.max(scores, axis=0, keepdims=True)
            probs = jnp.exp2(scores - top)
            probs = probs * (1.0 / jnp.sum(probs, axis=0, keepdims=True))
            probs_low = probs.astype(jnp.bfloat16)
            probs_kept[:, here] = probs_low
            attended = contract(values, probs_low, 0, 0)
            attended = attended.astype(jnp.bfloat16).astype(jnp.float32)
            da_here = da_cols[head, :, here]
            delta = jnp.sum(da_here.astype(jnp.float32) * attended, axis=0, keepdims=True)
            gate_term = jnp.sum(
                og_cols[head, :, here].astype(jnp.float32) * attended, axis=0, keepdims=True
            )
            for part in range(pair):
                term = gate_term[:, part * HD : (part + 1) * HD]
                gate_parts[head_id] += jnp.broadcast_to(term, (8, HD))
            d_probs = contract(values, da_here, 1, 0)
            scores_kept[head, :, here] = (probs * (d_probs - delta)).astype(jnp.bfloat16)
        d_values = contract(probs_kept[...], da_rows[head], 1, 0)
        d_keys = contract(scores_kept[head], q_rows[head], 1, 0) * factor
        both = jnp.concatenate([d_keys, d_values], axis=1)
        own_grad[head] = both[0:rows]
        g_out[head] = both[rows:].astype(jnp.bfloat16).reshape(spread, slot_rows, 2 * HD)
        each(lambda o: exchange(g_out, g_in, g_send, g_recv, head, o, lane_id).start())
        g_in[head, lane_id] = g_out[head, lane_id]

    def queries_grad(head):
        d_queries = contract(kv_all[head, :, 0:HD], scores_kept[head], 0, 0) * factor
        for index in range(group):
            at = pl.ds(pl.multiple_of(head * width + index * HD, HD), HD)
            dq_ref[:, at] = d_queries[:, index * HD : (index + 1) * HD].T.astype(jnp.bfloat16)

    def chain(head, way, step):
        return pltpu.make_async_remote_copy(
            src_ref=r_send_buf.at[head, way, step],
            dst_ref=r_recv_buf.at[head, way, step],
            send_sem=r_send.at[head, way, step],
            recv_sem=r_recv.at[head, way, step],
            device_id={"ctx": me + (spread if way == 0 else -spread)},
        )

    def chain_roles(way, step):
        if way == 0:
            owner = line_size - 1 - step
            return owner, place < owner, place == 0
        owner = step
        return owner, place > owner, place == line_size - 1

    def back(head):
        each(
            lambda o: exchange(
                g_out, g_in, g_send, g_recv, head, o, partner(spread - o)
            ).wait_recv()
        )
        flat = pick[...].reshape(remote_rows, line_size * rows)
        dense = contract(flat, g_in[head].reshape(remote_rows, 2 * HD), 0, 0)
        if line_size > 1:
            for step in range(line_size - 1):
                for way in range(2):
                    owner, passes, first = chain_roles(way, step)
                    mine = dense[owner * rows : (owner + 1) * rows]

                    @pl.when(passes & first)
                    def _():
                        r_send_buf[head, way, step] = mine.astype(jnp.bfloat16)
                        chain(head, way, step).start()

                    @pl.when(passes & jnp.logical_not(first))
                    def _():
                        chain(head, way, step).wait_recv()
                        r_send_buf[head, way, step] = (
                            mine + r_recv_buf[head, way, step].astype(jnp.float32)
                        ).astype(jnp.bfloat16)
                        chain(head, way, step).start()

                    @pl.when(place == owner)
                    def _():
                        chain(head, way, step).wait_recv()
                        own_grad[head] += r_recv_buf[head, way, step].astype(jnp.float32)
            for owner in range(line_size):
                @pl.when(place == owner)
                def _():
                    own_grad[head] += dense[owner * rows : (owner + 1) * rows]
        else:
            own_grad[head] += dense
        at = pl.ds(pl.multiple_of(head * HD, HD), HD)
        dk_ref[:, at] = own_grad[head, :, 0:HD].astype(jnp.bfloat16)
        dv_ref[:, at] = own_grad[head, :, HD:].astype(jnp.bfloat16)

    gate_parts[head_id] = jnp.zeros((8, HD), jnp.float32)
    if line_size > 1:
        def begin(head, carry):
            hop_start(head, 0)
            return carry

        lax.fori_loop(0, kv_count, begin, 0)
    else:
        def begin(head, carry):
            front(head)
            return carry

        lax.fori_loop(0, kv_count, begin, 0)

    build_bias()

    def get_ready(head, carry):
        prepare(head)
        return carry

    lax.fori_loop(0, kv_count, get_ready, 0)

    def turn(step, carry):
        if line_size > 1:
            @pl.when(step < kv_count)
            def _():
                front(step)

        @pl.when(step >= 1)
        def _():
            middle(step - 1)

        return carry

    lax.fori_loop(0, kv_count + 1, turn, 0)

    def gate_copy(offset, slot):
        return pltpu.make_async_remote_copy(
            src_ref=gate_parts.at[head_id],
            dst_ref=gate_parts.at[slot],
            send_sem=p_send.at[offset],
            recv_sem=p_recv.at[offset],
            device_id={"head": lax.rem(head_id + offset, head_peers)},
        )

    for offset in range(1, head_peers):
        gate_copy(offset, head_id).start()

    def queries_turn(head, carry):
        queries_grad(head)
        return carry

    def back_turn(head, carry):
        back(head)
        return carry

    lax.fori_loop(0, kv_count, queries_turn, 0)
    lax.fori_loop(0, kv_count, back_turn, 0)
    for offset in range(1, head_peers):
        gate_copy(offset, lax.rem(head_id + head_peers - offset, head_peers)).wait_recv()
    total = jnp.sum(gate_parts[...], axis=0)
    dgate_ref[...] = gate_row * (1.0 - gate_row) * total[0:1, :]

    for offset in range(1, head_peers):
        gate_copy(offset, head_id).wait_send()

    def finish(head, carry):
        each(lambda o: exchange(x_out, x_in, x_send, x_recv, head, o, lane_id).wait_send())
        each(lambda o: exchange(g_out, g_in, g_send, g_recv, head, o, lane_id).wait_send())
        for step in range(line_size - 1):
            hop_sent(head, step)
            for way in range(2):
                _, passes, _ = chain_roles(way, step)

                @pl.when(passes)
                def _():
                    chain(head, way, step).wait_send()

        return carry

    lax.fori_loop(0, kv_count, finish, 0)


def write(dq_in_ref, dk_in_ref, dv_in_ref, dgate_in_ref, dq_ref, dk_ref, dv_ref, dgate_ref):
    dq_ref[...] = dq_in_ref[...]
    dk_ref[...] = dk_in_ref[...]
    dv_ref[...] = dv_in_ref[...]
    dgate_ref[...] = dgate_in_ref[...]


def solution(mesh):
    peers = mesh.shape["ctx"]
    head_peers = mesh.shape["head"]
    line_size = LINE if peers % LINE == 0 else 1
    spread = peers // line_size

    def body(queries, key_rows, value_rows, out_grad, gate_logit, tile_plan, mask_kind):
        rows = queries.shape[0]
        kv_count = key_rows.shape[1] // HD
        width = queries.shape[1] // kv_count
        sections = tile_plan.shape[1]
        slot_rows = line_size * sections * TILE
        key_count = rows + spread * slot_rows
        hops = max(line_size - 1, 1)
        low, full = jnp.bfloat16, jnp.float32
        vmem = pl.BlockSpec(memory_space=pltpu.VMEM)
        dma = pltpu.SemaphoreType.DMA
        outs = pl.pallas_call(
            functools.partial(kernel, peers, line_size, head_peers),
            out_shape=(
                jax.ShapeDtypeStruct(queries.shape, low),
                jax.ShapeDtypeStruct(key_rows.shape, low),
                jax.ShapeDtypeStruct(value_rows.shape, low),
                jax.ShapeDtypeStruct((1, rows), full),
            ),
            in_specs=[vmem] * 7,
            out_specs=(vmem,) * 4,
            scratch_shapes=[
                pltpu.VMEM((spread, slot_rows, line_size * rows), low),
                pltpu.VMEM((key_count, rows), full),
                pltpu.VMEM((kv_count, line_size, rows, 2 * HD), low),
                pltpu.VMEM((kv_count, spread, slot_rows, 2 * HD), low),
                pltpu.VMEM((kv_count, spread, slot_rows, 2 * HD), low),
                pltpu.VMEM((kv_count, spread, slot_rows, 2 * HD), low),
                pltpu.VMEM((kv_count, spread, slot_rows, 2 * HD), low),
                pltpu.VMEM((kv_count, rows, 2 * HD), full),
                pltpu.VMEM((kv_count, width, HD), low),
                pltpu.VMEM((kv_count, HD, width), low),
                pltpu.VMEM((kv_count, width, HD), low),
                pltpu.VMEM((kv_count, HD, width), low),
                pltpu.VMEM((kv_count, HD, width), low),
                pltpu.VMEM((kv_count, key_count, 2 * HD), low),
                pltpu.VMEM((key_count, width), low),
                pltpu.VMEM((kv_count, key_count, width), low),
                pltpu.VMEM((head_peers, 8, rows), full),
                pltpu.VMEM((kv_count, 2, hops, rows, 2 * HD), low),
                pltpu.VMEM((kv_count, 2, hops, rows, 2 * HD), low),
                dma((kv_count, spread)),
                dma((kv_count, spread)),
                dma((kv_count, spread)),
                dma((kv_count, spread)),
                dma((kv_count, 2, hops)),
                dma((kv_count, 2, hops)),
                dma((kv_count, 2, hops)),
                dma((kv_count, 2, hops)),
                dma((head_peers,)),
                dma((head_peers,)),
            ],
            compiler_params=pltpu.CompilerParams(
                collective_id=0, has_side_effects=True, vmem_limit_bytes=56 * 1024 * 1024
            ),
            name="attention_grad",
        )(
            queries,
            key_rows,
            value_rows,
            out_grad,
            gate_logit.reshape(1, rows),
            tile_plan,
            mask_kind,
        )
        outs = pl.pallas_call(
            write,
            out_shape=(
                jax.ShapeDtypeStruct(queries.shape, low),
                jax.ShapeDtypeStruct(key_rows.shape, low),
                jax.ShapeDtypeStruct(value_rows.shape, low),
                jax.ShapeDtypeStruct((1, rows), full),
            ),
            in_specs=[vmem] * 4,
            out_specs=(vmem,) * 4,
            name="write_grads",
        )(*outs)
        return outs[0], outs[1], outs[2], outs[3].reshape(rows)

    return jax.shard_map(
        body,
        mesh=mesh,
        in_specs=(
            P("ctx", "head"),
            P("ctx", "head"),
            P("ctx", "head"),
            P("ctx", "head"),
            P("ctx"),
            P(),
            P("ctx", None, None),
        ),
        out_specs=(P("ctx", "head"), P("ctx", "head"), P("ctx", "head"), P("ctx")),
        check_vma=False,
    )
```

```python
import functools
import math

import jax
import jax.numpy as jnp
from jax import lax
from jax.experimental import pallas as pl
from jax.experimental.pallas import tpu as pltpu
from jax.sharding import PartitionSpec as P

HD = 128
TILE = 8
LINE = 1

NEG = -1e30


def contract(a, b, dim_a, dim_b):
    return lax.dot_general(
        a, b, (((dim_a,), (dim_b,)), ((), ())), preferred_element_type=jnp.float32
    )


def kernel(
    peers,
    line_size,
    head_peers,
    q_ref,
    k_ref,
    v_ref,
    og_ref,
    gate_row_ref,
    plan_ref,
    kind_ref,
    dq_ref,
    dk_ref,
    dv_ref,
    dgate_ref,
    pick,
    bias,
    line,
    x_out,
    x_in,
    g_out,
    g_in,
    own_grad,
    q_rows,
    q_cols,
    da_rows,
    da_cols,
    og_cols,
    kv_all,
    probs_kept,
    scores_kept,
    gate_parts,
    r_send_buf,
    r_recv_buf,
    x_send,
    x_recv,
    g_send,
    g_recv,
    l_send,
    l_recv,
    r_send,
    r_recv,
    p_send,
    p_recv,
):
    rows = q_ref.shape[0]
    kv_count = k_ref.shape[1] // HD
    group = q_ref.shape[1] // k_ref.shape[1]
    width = group * HD
    sections = plan_ref.shape[1]
    spread = peers // line_size
    slot_rows = line_size * sections * TILE
    remote_rows = spread * slot_rows
    factor = 1.0 / math.sqrt(HD)
    me = lax.axis_index("ctx")
    place = me // spread
    lane_id = lax.rem(me, spread)
    head_id = lax.axis_index("head")

    def partner(offset):
        return lax.rem(lane_id + offset, spread)

    barrier = pltpu.get_barrier_semaphore()

    def greet(offset, carry):
        pl.semaphore_signal(barrier, inc=1, device_id={"ctx": place * spread + partner(offset)})
        return carry

    lax.fori_loop(1, spread, greet, 0)
    for offset in range(1, head_peers):
        pl.semaphore_signal(
            barrier, inc=1, device_id={"head": lax.rem(head_id + offset, head_peers)}
        )
    if line_size > 1:
        @pl.when(place > 0)
        def _():
            pl.semaphore_signal(barrier, inc=1, device_id={"ctx": me - spread})

        @pl.when(place < line_size - 1)
        def _():
            pl.semaphore_signal(barrier, inc=1, device_id={"ctx": me + spread})

    def columns(plan_rows, which):
        row = lax.broadcasted_iota(jnp.int32, (slot_rows, peers), 0)
        lane = lax.broadcasted_iota(jnp.int32, (slot_rows, peers), 1)
        hit = lane == (row // (sections * TILE)) * spread + which
        section = (row // TILE) % sections
        total = jnp.zeros((slot_rows, peers), jnp.float32)
        for index in range(sections):
            total = total + jnp.where(
                hit & (section == index), plan_rows[index : index + 1, :], 0.0
            )
        return jnp.sum(total, axis=1, keepdims=True)

    def build_pick(which, carry):
        plan_rows = plan_ref[place * spread + which].astype(jnp.float32)
        tile = columns(plan_rows, lane_id).astype(jnp.int32)
        shape = (slot_rows, line_size * rows)
        row = lax.broadcasted_iota(jnp.int32, shape, 0)
        lane = lax.broadcasted_iota(jnp.int32, shape, 1)
        target = (row // (sections * TILE)) * rows + tile * TILE + row % TILE
        pick[which] = jnp.where((tile >= 0) & (lane == target), 1.0, 0.0).astype(jnp.bfloat16)
        return carry

    lax.fori_loop(0, spread, build_pick, 0)

    def fill(head, carry):
        at = pl.ds(pl.multiple_of(head * HD, HD), HD)
        line[head, place] = jnp.concatenate([k_ref[:, at], v_ref[:, at]], axis=1)
        return carry

    lax.fori_loop(0, kv_count, fill, 0)

    below = (place + line_size - 1) // line_size
    above = (2 * (line_size - 1) - place) // line_size
    pl.semaphore_wait(barrier, spread - 1 + head_peers - 1 + below + above)

    def hop(head, way, step, origin):
        return pltpu.make_async_remote_copy(
            src_ref=line.at[head, origin],
            dst_ref=line.at[head, origin],
            send_sem=l_send.at[head, way, step],
            recv_sem=l_recv.at[head, way, step],
            device_id={"ctx": me + (spread if way == 0 else -spread)},
        )

    def hop_start(head, step):
        @pl.when((place >= step) & (place < line_size - 1))
        def _():
            hop(head, 0, step, place - step).start()

        @pl.when((place + step <= line_size - 1) & (place > 0))
        def _():
            hop(head, 1, step, place + step).start()

    def hop_wait(head, step):
        @pl.when(place - 1 - step >= 0)
        def _():
            hop(head, 0, step, place - 1 - step).wait_recv()

        @pl.when(place + 1 + step <= line_size - 1)
        def _():
            hop(head, 1, step, place + 1 + step).wait_recv()

    def hop_sent(head, step):
        @pl.when((place >= step) & (place < line_size - 1))
        def _():
            hop(head, 0, step, place - step).wait_send()

        @pl.when((place + step <= line_size - 1) & (place > 0))
        def _():
            hop(head, 1, step, place + step).wait_send()

    def exchange(source, target, send, recv, head, offset, slot):
        return pltpu.make_async_remote_copy(
            src_ref=source.at[head, partner(offset)],
            dst_ref=target.at[head, slot],
            send_sem=send.at[head, offset],
            recv_sem=recv.at[head, offset],
            device_id={"ctx": place * spread + partner(offset)},
        )

    def each(body):
        def step(turn, carry):
            body(spread // 2 + (turn // 2) * (1 - 2 * lax.rem(turn, 2)))
            return carry

        lax.fori_loop(1, spread, step, 0)

    def front(head):
        for step in range(line_size - 1):
            hop_wait(head, step)
            if step + 1 < line_size - 1:
                hop_start(head, step + 1)
        flat = pick[...].reshape(remote_rows, line_size * rows)
        chosen = contract(flat, line[head].reshape(line_size * rows, 2 * HD), 1, 0)
        x_out[head] = chosen.astype(jnp.bfloat16).reshape(spread, slot_rows, 2 * HD)
        each(lambda o: exchange(x_out, x_in, x_send, x_recv, head, o, lane_id).start())
        x_in[head, lane_id] = x_out[head, lane_id]

    gate_row = jax.nn.sigmoid(gate_row_ref[...])
    gate_col = jnp.broadcast_to(gate_row, (HD, rows)).T

    def prepare(head):
        for index in range(group):
            at = pl.ds(pl.multiple_of(head * width + index * HD, HD), HD)
            here = slice(index * HD, (index + 1) * HD)
            query = q_ref[:, at]
            grad = og_ref[:, at].astype(jnp.float32)
            grad_col = grad.T
            q_rows[head, here, :] = query
            q_cols[head, :, here] = query.astype(jnp.float32).T.astype(jnp.bfloat16)
            og_cols[head, :, here] = grad_col.astype(jnp.bfloat16)
            da_rows[head, here, :] = (gate_col * grad).astype(jnp.bfloat16)
            da_cols[head, :, here] = (gate_row * grad_col).astype(jnp.bfloat16)

    def build_bias():
        late = (
            lax.broadcasted_iota(jnp.int32, (slot_rows, rows), 1) >= rows // 2
        ).astype(jnp.float32)
        own_row = lax.broadcasted_iota(jnp.int32, (rows, rows), 0)
        own_lane = lax.broadcasted_iota(jnp.int32, (rows, rows), 1)
        bias[0:rows, :] = jnp.where(own_row <= own_lane, 0.0, NEG)
        seen = jnp.where(
            plan_ref[me] >= 0, 2.0 - kind_ref[0].astype(jnp.float32), 0.0
        )
        for which in range(spread):
            code = columns(seen, which)
            start = rows + which * slot_rows
            bias[start : start + slot_rows, :] = jnp.where(code + late >= 2.0, 0.0, NEG)

    pair = 2 if group % 2 == 0 else 1
    pair_width = pair * HD

    def middle(head):
        each(
            lambda o: exchange(
                x_out, x_in, x_send, x_recv, head, o, partner(spread - o)
            ).wait_recv()
        )
        kv_all[head, 0:rows, :] = line[head, place]
        kv_all[head, rows:, :] = x_in[head].reshape(remote_rows, 2 * HD)
        keys = kv_all[head, :, 0:HD]
        values = kv_all[head, :, HD:]
        mask = jnp.concatenate([bias[...]] * pair, axis=1)
        for index in range(group // pair):
            here = slice(index * pair_width, (index + 1) * pair_width)
            scores = contract(keys, q_cols[head, :, here], 1, 0)
            scores = scores * (factor * math.log2(math.e)) + mask
            top = jnp.max(scores, axis=0, keepdims=True)
            probs = jnp.exp2(scores - top)
            probs = probs * (1.0 / jnp.sum(probs, axis=0, keepdims=True))
            probs_low = probs.astype(jnp.bfloat16)
            probs_kept[:, here] = probs_low
            attended = contract(values, probs_low, 0, 0)
            attended = attended.astype(jnp.bfloat16).astype(jnp.float32)
            da_here = da_cols[head, :, here]
            delta = jnp.sum(da_here.astype(jnp.float32) * attended, axis=0, keepdims=True)
            gate_term = jnp.sum(
                og_cols[head, :, here].astype(jnp.float32) * attended, axis=0, keepdims=True
            )
            for part in range(pair):
                term = gate_term[:, part * HD : (part + 1) * HD]
                gate_parts[head_id] += jnp.broadcast_to(term, (8, HD))
            d_probs = contract(values, da_here, 1, 0)
            scores_kept[head, :, here] = (probs * (d_probs - delta)).astype(jnp.bfloat16)
        d_values = contract(probs_kept[...], da_rows[head], 1, 0)
        d_keys = contract(scores_kept[head], q_rows[head], 1, 0) * factor
        both = jnp.concatenate([d_keys, d_values], axis=1)
        own_grad[head] = both[0:rows]
        g_out[head] = both[rows:].astype(jnp.bfloat16).reshape(spread, slot_rows, 2 * HD)
        each(lambda o: exchange(g_out, g_in, g_send, g_recv, head, o, lane_id).start())
        g_in[head, lane_id] = g_out[head, lane_id]

    def queries_grad(head):
        d_queries = contract(kv_all[head, :, 0:HD], scores_kept[head], 0, 0) * factor
        for index in range(group):
            at = pl.ds(pl.multiple_of(head * width + index * HD, HD), HD)
            dq_ref[:, at] = d_queries[:, index * HD : (index + 1) * HD].T.astype(jnp.bfloat16)

    def chain(head, way, step):
        return pltpu.make_async_remote_copy(
            src_ref=r_send_buf.at[head, way, step],
            dst_ref=r_recv_buf.at[head, way, step],
            send_sem=r_send.at[head, way, step],
            recv_sem=r_recv.at[head, way, step],
            device_id={"ctx": me + (spread if way == 0 else -spread)},
        )

    def chain_roles(way, step):
        if way == 0:
            owner = line_size - 1 - step
            return owner, place < owner, place == 0
        owner = step
        return owner, place > owner, place == line_size - 1

    def back(head):
        each(
            lambda o: exchange(
                g_out, g_in, g_send, g_recv, head, o, partner(spread - o)
            ).wait_recv()
        )
        flat = pick[...].reshape(remote_rows, line_size * rows)
        dense = contract(flat, g_in[head].reshape(remote_rows, 2 * HD), 0, 0)
        if line_size > 1:
            for step in range(line_size - 1):
                for way in range(2):
                    owner, passes, first = chain_roles(way, step)
                    mine = dense[owner * rows : (owner + 1) * rows]

                    @pl.when(passes & first)
                    def _():
                        r_send_buf[head, way, step] = mine.astype(jnp.bfloat16)
                        chain(head, way, step).start()

                    @pl.when(passes & jnp.logical_not(first))
                    def _():
                        chain(head, way, step).wait_recv()
                        r_send_buf[head, way, step] = (
                            mine + r_recv_buf[head, way, step].astype(jnp.float32)
                        ).astype(jnp.bfloat16)
                        chain(head, way, step).start()

                    @pl.when(place == owner)
                    def _():
                        chain(head, way, step).wait_recv()
                        own_grad[head] += r_recv_buf[head, way, step].astype(jnp.float32)
            for owner in range(line_size):
                @pl.when(place == owner)
                def _():
                    own_grad[head] += dense[owner * rows : (owner + 1) * rows]
        else:
            own_grad[head] += dense
        at = pl.ds(pl.multiple_of(head * HD, HD), HD)
        dk_ref[:, at] = own_grad[head, :, 0:HD].astype(jnp.bfloat16)
        dv_ref[:, at] = own_grad[head, :, HD:].astype(jnp.bfloat16)

    gate_parts[head_id] = jnp.zeros((8, HD), jnp.float32)
    if line_size > 1:
        def begin(head, carry):
            hop_start(head, 0)
            return carry

        lax.fori_loop(0, kv_count, begin, 0)
    else:
        def begin(head, carry):
            front(head)
            return carry

        lax.fori_loop(0, kv_count, begin, 0)

    build_bias()

    def get_ready(head, carry):
        prepare(head)
        return carry

    lax.fori_loop(0, kv_count, get_ready, 0)

    def turn(step, carry):
        if line_size > 1:
            @pl.when(step < kv_count)
            def _():
                front(step)

        @pl.when(step >= 1)
        def _():
            middle(step - 1)

        return carry

    lax.fori_loop(0, kv_count + 1, turn, 0)

    def gate_copy(offset, slot):
        return pltpu.make_async_remote_copy(
            src_ref=gate_parts.at[head_id],
            dst_ref=gate_parts.at[slot],
            send_sem=p_send.at[offset],
            recv_sem=p_recv.at[offset],
            device_id={"head": lax.rem(head_id + offset, head_peers)},
        )

    for offset in range(1, head_peers):
        gate_copy(offset, head_id).start()

    def queries_turn(head, carry):
        queries_grad(head)
        return carry

    def back_turn(head, carry):
        back(head)
        return carry

    lax.fori_loop(0, kv_count, queries_turn, 0)
    lax.fori_loop(0, kv_count, back_turn, 0)
    for offset in range(1, head_peers):
        gate_copy(offset, lax.rem(head_id + head_peers - offset, head_peers)).wait_recv()
    total = jnp.sum(gate_parts[...], axis=0)
    dgate_ref[...] = gate_row * (1.0 - gate_row) * total[0:1, :]

    for offset in range(1, head_peers):
        gate_copy(offset, head_id).wait_send()

    def finish(head, carry):
        each(lambda o: exchange(x_out, x_in, x_send, x_recv, head, o, lane_id).wait_send())
        each(lambda o: exchange(g_out, g_in, g_send, g_recv, head, o, lane_id).wait_send())
        for step in range(line_size - 1):
            hop_sent(head, step)
            for way in range(2):
                _, passes, _ = chain_roles(way, step)

                @pl.when(passes)
                def _():
                    chain(head, way, step).wait_send()

        return carry

    lax.fori_loop(0, kv_count, finish, 0)


def write(dq_in_ref, dk_in_ref, dv_in_ref, dgate_in_ref, dq_ref, dk_ref, dv_ref, dgate_ref):
    dq_ref[...] = dq_in_ref[...]
    dk_ref[...] = dk_in_ref[...]
    dv_ref[...] = dv_in_ref[...]
    dgate_ref[...] = dgate_in_ref[...]


def solution(mesh):
    peers = mesh.shape["ctx"]
    head_peers = mesh.shape["head"]
    line_size = LINE if peers % LINE == 0 else 1
    spread = peers // line_size

    def body(queries, key_rows, value_rows, out_grad, gate_logit, tile_plan, mask_kind):
        rows = queries.shape[0]
        kv_count = key_rows.shape[1] // HD
        width = queries.shape[1] // kv_count
        sections = tile_plan.shape[1]
        slot_rows = line_size * sections * TILE
        key_count = rows + spread * slot_rows
        hops = max(line_size - 1, 1)
        low, full = jnp.bfloat16, jnp.float32
        vmem = pl.BlockSpec(memory_space=pltpu.VMEM)
        dma = pltpu.SemaphoreType.DMA
        outs = pl.pallas_call(
            functools.partial(kernel, peers, line_size, head_peers),
            out_shape=(
                jax.ShapeDtypeStruct(queries.shape, low),
                jax.ShapeDtypeStruct(key_rows.shape, low),
                jax.ShapeDtypeStruct(value_rows.shape, low),
                jax.ShapeDtypeStruct((1, rows), full),
            ),
            in_specs=[vmem] * 7,
            out_specs=(vmem,) * 4,
            scratch_shapes=[
                pltpu.VMEM((spread, slot_rows, line_size * rows), low),
                pltpu.VMEM((key_count, rows), full),
                pltpu.VMEM((kv_count, line_size, rows, 2 * HD), low),
                pltpu.VMEM((kv_count, spread, slot_rows, 2 * HD), low),
                pltpu.VMEM((kv_count, spread, slot_rows, 2 * HD), low),
                pltpu.VMEM((kv_count, spread, slot_rows, 2 * HD), low),
                pltpu.VMEM((kv_count, spread, slot_rows, 2 * HD), low),
                pltpu.VMEM((kv_count, rows, 2 * HD), full),
                pltpu.VMEM((kv_count, width, HD), low),
                pltpu.VMEM((kv_count, HD, width), low),
                pltpu.VMEM((kv_count, width, HD), low),
                pltpu.VMEM((kv_count, HD, width), low),
                pltpu.VMEM((kv_count, HD, width), low),
                pltpu.VMEM((kv_count, key_count, 2 * HD), low),
                pltpu.VMEM((key_count, width), low),
                pltpu.VMEM((kv_count, key_count, width), low),
                pltpu.VMEM((head_peers, 8, rows), full),
                pltpu.VMEM((kv_count, 2, hops, rows, 2 * HD), low),
                pltpu.VMEM((kv_count, 2, hops, rows, 2 * HD), low),
                dma((kv_count, spread)),
                dma((kv_count, spread)),
                dma((kv_count, spread)),
                dma((kv_count, spread)),
                dma((kv_count, 2, hops)),
                dma((kv_count, 2, hops)),
                dma((kv_count, 2, hops)),
                dma((kv_count, 2, hops)),
                dma((head_peers,)),
                dma((head_peers,)),
            ],
            compiler_params=pltpu.CompilerParams(
                collective_id=0, has_side_effects=True, vmem_limit_bytes=56 * 1024 * 1024
            ),
            name="attention_grad",
        )(
            queries,
            key_rows,
            value_rows,
            out_grad,
            gate_logit.reshape(1, rows),
            tile_plan,
            mask_kind,
        )
        outs = pl.pallas_call(
            write,
            out_shape=(
                jax.ShapeDtypeStruct(queries.shape, low),
                jax.ShapeDtypeStruct(key_rows.shape, low),
                jax.ShapeDtypeStruct(value_rows.shape, low),
                jax.ShapeDtypeStruct((1, rows), full),
            ),
            in_specs=[vmem] * 4,
            out_specs=(vmem,) * 4,
            name="write_grads",
        )(*outs)
        return outs[0], outs[1], outs[2], outs[3].reshape(rows)

    return jax.shard_map(
        body,
        mesh=mesh,
        in_specs=(
            P("ctx", "head"),
            P("ctx", "head"),
            P("ctx", "head"),
            P("ctx", "head"),
            P("ctx"),
            P(),
            P("ctx", None, None),
        ),
        out_specs=(P("ctx", "head"), P("ctx", "head"), P("ctx", "head"), P("ctx")),
        check_vma=False,
    )
```
